128 devices in a mesh: ctx: 8 (over z, core), ch: 16 (over y, x).
Axes of the slice: x: 4, y: 4, z: 4, core: 2. Of those that a mesh axis runs over, the one named last changes fastest.
Arguments:
- x_owned: bfloat16 [8192, 8192], P('ctx', 'ch'), may hold values from -40 to 40
- live_blocks: int32 [8], replicated, may hold values from 0 to 8, as said below
- seq_lengths: int32 [3], replicated, may hold values from 1 to 2048, as said below
- norm_gain: float32 [8192], replicated, may hold values from 0.5 to 1.5
- w_in: bfloat16 [3, 8192, 4096], P(None, None, 'ch'), may hold values from -0.0625 to 0.0625
- w_short: float32 [3, 3, 4096], P(None, None, 'ch'), may hold values from -2.5 to 2.5
- decay_rates: float32 [16, 4096], P(None, 'ch'), may hold values from 4.8828125e-06 to 0.03
- residues: float32 [16, 4096], P(None, 'ch'), may hold values from -1.5 to 1.5
- skip_gain: float32 [4096], P('ch'), may hold values from 0.5 to 1.5
- w_out: bfloat16 [4096, 8192], P('ch'), may hold values from -0.09375 to 0.09375
Outputs:
- out: bfloat16 [8192, 4096], P('ch', 'ctx')
The draws below stay inside these ranges and needn't reach their ends.
Inputs may be any that keep to these rules, and one draw needn't show every extreme that they name: `live_blocks`: the counts sum to 32. The live blocks of buffers 0 .. s - 1 number s * 4 + e with e between -2 and 2, and both ends occur. Rows of a buffer past its live blocks are never read. `seq_lengths`: the lengths sum to 4096.
All inputs are finite; a program needn't handle non-finite values.
Results may differ from the reference program's by a relative error of at most 0.02.
Values may be sent and summed in bfloat16 or wider, within the bound.
A program may use at most 128 MiB of HBM per device.

```python
import jax
import jax.numpy as jnp
from jax import lax

D = 8192
HC = 4096
MODES = 16
TAPS = 3
BLOCK = 128
BLK_DEV = 4
TOKENS = 4096
OWNERS = 8
SHARDS = 16
SLOTS = 8192


def draw_x_owned(key, part):
    key = jax.random.fold_in(key, 3)
    base_key, row_key, col_key = jax.random.split(key, 3)
    ramp = jnp.arange(D, dtype=jnp.float32) / D
    base = jnp.clip(jax.random.normal(base_key, (SLOTS, D), jnp.float32), -4.0, 4.0)
    low_end = 0.3
    high_end = 3.0
    rise_end = 3.0
    row_scale = low_end * (high_end / low_end) ** jax.random.uniform(row_key, (SLOTS, 1), jnp.float32)
    col_scale = low_end * (high_end / low_end) ** jax.random.uniform(col_key, (1, D), jnp.float32)
    return jnp.clip(base * row_scale * col_scale * rise_end ** ramp, -40.0, 40.0).astype(jnp.bfloat16)


def draw_live_blocks(key, part):
    key = jax.random.fold_in(key, 7)
    first_key, second_key = jax.random.split(key)
    half_span = BLK_DEV // 2
    drift = jax.random.randint(first_key, (OWNERS,), -half_span, half_span + 1).astype(jnp.int32)
    picked = jax.random.randint(second_key, (), 1, OWNERS - 1).astype(jnp.int32)
    owner_index = jnp.arange(OWNERS, dtype=jnp.int32)
    drift = jnp.where(owner_index == picked, half_span, jnp.where(owner_index == picked - 1, -half_span, drift))
    drift = jnp.where(owner_index == OWNERS - 1, 0, drift).astype(jnp.int32)
    drift_before = jnp.concatenate([jnp.zeros((1,), jnp.int32), drift[:-1]])
    return (BLK_DEV + drift - drift_before).astype(jnp.int32)


def draw_seq_lengths(key, part):
    key = jax.random.fold_in(key, 13)
    split_key, place_key = jax.random.split(key)
    longest = TOKENS // 2
    remain = TOKENS - longest
    first_part = jax.random.randint(split_key, (), 1, remain).astype(jnp.int32)
    second_part = (remain - first_part).astype(jnp.int32)
    stacked = jnp.stack([jnp.array(longest, jnp.int32), first_part, second_part]).astype(jnp.int32)
    place = jax.random.randint(place_key, (), 0, 3).astype(jnp.int32)
    return jnp.roll(stacked, place).astype(jnp.int32)


def draw_decay_rates(key, part):
    key = jax.random.fold_in(key, 11)
    low_end = 0.02 / TOKENS
    high_end = 0.03
    spot = jax.random.uniform(key, (MODES, HC), jnp.float32)
    return (low_end * (high_end / low_end) ** spot).astype(jnp.float32)


def level_of(stream_key, dims, cuts, smallest, largest):
    loudness, own = 1.0, jax.random.fold_in(stream_key, 6)
    for dim, shards_of in cuts:
        heights = jnp.exp(jax.random.uniform(jax.random.fold_in(own, dim), (shards_of,), jnp.float32, smallest / len(cuts), largest / len(cuts)))
        loudness = loudness * jnp.repeat(heights, dims[dim] // shards_of).reshape([-1 if axis == dim else 1 for axis in range(len(dims))])
    return loudness


def scatter_about(own_key, dims, spread, bound, cuts=(), kind=jnp.bfloat16):
    gain = level_of(own_key, dims, cuts, -0.22, 0.18) if cuts else 1.0
    values = jax.random.normal(own_key, dims, jnp.float32) * spread * gain
    return jnp.minimum(jnp.maximum(values, -bound), bound).astype(kind)


def setup_inputs(seed: int = 0) -> dict:
    arg_keys = jax.random.split(jax.random.key(seed), 11)
    return {
        "x_owned": draw_x_owned(jax.random.fold_in(arg_keys[10], 71), 0),
        "live_blocks": draw_live_blocks(jax.random.fold_in(arg_keys[10], 71), 0),
        "seq_lengths": draw_seq_lengths(jax.random.fold_in(arg_keys[10], 71), 0),
        "norm_gain": jnp.clip(1.0 + 0.1 * jax.random.normal(arg_keys[3], (D,), jnp.float32), 0.5, 1.5),
        "w_in": scatter_about(arg_keys[4], (3, D, HC), D ** -0.5, 0.0625, ((2, 16),)),
        "w_short": scatter_about(arg_keys[5], (TAPS, 3, HC), 0.6, 2.5, ((2, 16),), jnp.float32),
        "decay_rates": draw_decay_rates(jax.random.fold_in(arg_keys[10], 71), 0),
        "residues": scatter_about(arg_keys[7], (MODES, HC), MODES ** -0.5, 1.5, ((1, 16),), jnp.float32),
        "skip_gain": jnp.clip(0.5 + 1.0 * jax.random.uniform(arg_keys[8], (HC,), jnp.float32) ** level_of(arg_keys[8], (HC,), ((0, 16),), -0.2, 0.2), 0.5, 1.5),
        "w_out": scatter_about(arg_keys[9], (HC, D), HC ** -0.5, 0.09375, ((0, 16),)),
    }


EPS = 1e-06

def packed_window(x_owned, live_blocks):
    capacity = 2 * BLK_DEV
    ends_at = jnp.cumsum(live_blocks).astype(jnp.int32)
    starts_at = (ends_at - live_blocks).astype(jnp.int32)
    block_index = jnp.arange(TOKENS // BLOCK, dtype=jnp.int32)
    owner_index = lax.optimization_barrier(jnp.sum((block_index[:, None] >= ends_at[None, :]).astype(jnp.int32), axis=1)).astype(jnp.int32)
    slot_index = (block_index - starts_at[owner_index]).astype(jnp.int32)
    source = (owner_index * capacity + slot_index).astype(jnp.int32)
    block_rows = x_owned.reshape(OWNERS * capacity, BLOCK, D)
    return jnp.take(block_rows, source, axis=0).reshape(TOKENS, D)

def segment_of(seq_lengths, positions):
    ends_at = jnp.cumsum(seq_lengths).astype(jnp.int32)
    inside = lax.optimization_barrier(jnp.sum((positions[:, None] >= ends_at[None, :]).astype(jnp.int32), axis=1)).astype(jnp.int32)
    return jnp.where(positions < 0, -1, inside).astype(jnp.int32)

def reference(x_owned, live_blocks, seq_lengths, norm_gain, w_in, w_short, decay_rates, residues, skip_gain, w_out):
    window = packed_window(x_owned, live_blocks)
    widened = window.astype(jnp.float32)
    row_scale = lax.rsqrt(lax.optimization_barrier(jnp.mean(widened * widened, axis=1, keepdims=True)) + EPS)
    normed = (widened * row_scale * norm_gain[None, :]).astype(jnp.bfloat16)
    projected = jnp.stack([jnp.dot(normed, w_in[branch_index], preferred_element_type=jnp.float32) for branch_index in range(3)]).astype(jnp.bfloat16)
    positions = jnp.arange(TOKENS, dtype=jnp.int32)
    segment = segment_of(seq_lengths, positions)
    padded = jnp.pad(projected.astype(jnp.float32), ((0, 0), (TAPS - 1, 0), (0, 0)))
    segment_padded = segment_of(seq_lengths, jnp.arange(-(TAPS - 1), TOKENS, dtype=jnp.int32))
    features = jnp.zeros((3, TOKENS, HC), jnp.float32)
    for tap_index in range(TAPS):
        begin_at = TAPS - 1 - tap_index
        same_seq = (segment_padded[begin_at:begin_at + TOKENS] == segment).astype(jnp.float32)
        features = features + w_short[tap_index][:, None, :] * padded[:, begin_at:begin_at + TOKENS, :] * same_seq[None, :, None]
    query_part = features[0]
    gated_input = features[1] * features[2]
    decay = jnp.exp(-decay_rates)
    mode_weight = decay_rates * 0.0 + residues * jnp.sqrt(-jnp.expm1(-2.0 * decay_rates))
    is_start = jnp.concatenate([jnp.ones((1,), jnp.float32), (segment[1:] != segment[:-1]).astype(jnp.float32)])

    def advance(state_now, token_in):
        token_value, start_flag = token_in
        state_now = decay * state_now * (1.0 - start_flag) + token_value[None, :]
        return (state_now, lax.optimization_barrier(jnp.sum(mode_weight * state_now, axis=0)))
    state_zero = jnp.zeros((MODES, HC), jnp.float32)
    final_state, convolved = lax.scan(advance, state_zero, (gated_input, is_start))
    mixed = convolved + skip_gain[None, :] * gated_input
    gated_out = (query_part * mixed).astype(jnp.bfloat16)
    shard_width = HC // SHARDS
    summed = jnp.zeros((TOKENS, D), jnp.float32)
    for shard_index in range(SHARDS):
        partial_value = jnp.dot(gated_out[:, shard_index * shard_width:(shard_index + 1) * shard_width], w_out[shard_index * shard_width:(shard_index + 1) * shard_width], preferred_element_type=jnp.float32)
        summed = summed + lax.optimization_barrier(partial_value.astype(jnp.bfloat16)).astype(jnp.float32)
    return summed.T.astype(jnp.bfloat16)
```

```python
import functools

import jax
import jax.numpy as jnp
from jax import lax
from jax.experimental import pallas as pl
from jax.experimental.pallas import tpu as pltpu
from jax.sharding import PartitionSpec as P

EPS = 1e-06
TAPS = 3
BRANCHES = 3
SIDE = 4
LANES = 128
GROUPS = 8
MESH = pl.DeviceIdType.MESH


def remote(src, dst, send_sem, recv_sem, device):
    return pltpu.make_async_remote_copy(
        src_ref=src,
        dst_ref=dst,
        send_sem=send_sem,
        recv_sem=recv_sem,
        device_id=device,
        device_id_type=MESH,
    )


def each(lower, upper, step):
    def run(index, carry):
        step(index)
        return carry

    lax.fori_loop(lower, upper, run, 0)


def plane_gather(buf, send_sems, recv_sems, ctx, row, col, use):
    half = buf.shape[2]
    quarter = half // 2
    rows = (pl.ds(0, half), pl.ds(0, half), pl.ds(0, quarter), pl.ds(quarter, quarter))

    def place(h, first, second):
        x = lax.rem(col + (1 - h) * first + h * second + 2 * SIDE, SIDE)
        y = lax.rem(row + (1 - h) * second + h * first + 2 * SIDE, SIDE)
        return y * SIDE + x

    def offset(ring):
        k = ring - 1
        return k + k // 2 - 2 * (k // 3)

    def piece(ring, h, along):
        if isinstance(ring, int) and ring == 0:
            return place(h, along, 0)
        return place(h, offset(ring), along)

    def neighbour(ring, h, along):
        if isinstance(ring, int) and ring == 0:
            return (ctx, place(h, along, 0))
        return (ctx, place(h, 0, along))

    def copy(ring, h, kind, along):
        part = buf.at[piece(ring, h, along), h, rows[kind]]
        return remote(
            part,
            part,
            send_sems.at[ring, h, kind],
            recv_sems.at[ring, h, kind],
            neighbour(ring, h, 1 - 2 * (kind % 2)),
        )

    def send(ring, h):
        copy(ring, h, 0, 0).start()
        copy(ring, h, 1, 0).start()

    def forward(ring, h):
        copy(ring, h, 0, -1).wait_recv()
        copy(ring, h, 2, -1).start()
        copy(ring, h, 1, 1).wait_recv()
        copy(ring, h, 3, 1).start()

    def finish(ring, h):
        copy(ring, h, 2, 2).wait_recv()
        copy(ring, h, 3, 2).wait_recv()

    def open_rings(h):
        send(0, h)
        send(1, h)

    def grow(h):
        forward(0, h)
        send(2, h)
        send(3, h)

    def close_first(h):
        finish(0, h)
        send(4, h)

    each(0, 2, open_rings)
    each(0, 2, lambda h: use(h, place(h, 0, 0)))
    each(0, 2, grow)
    each(0, 4, lambda i: use(i // 2, piece(0, i // 2, 2 * (i % 2) - 1)))
    each(0, 2, close_first)
    each(0, 2, lambda h: use(h, piece(0, h, 2)))

    def pass_on(ring):
        each(0, 2, lambda h: forward(ring, h))
        each(0, 4, lambda i: use(i // 2, piece(ring, i // 2, 2 * (i % 2) - 1)))

    def take_last(ring):
        each(0, 2, lambda h: finish(ring, h))
        each(0, 2, lambda h: use(h, piece(ring, h, 2)))

    each(1, SIDE + 1, pass_on)
    each(1, SIDE + 1, take_last)

    def drain(index):
        h = index % 2
        for kind in range(4):
            copy(0, h, kind, 0).wait_send()
        each(1, SIDE + 1, lambda ring: drain_ring(ring, h))

    def drain_ring(ring, h):
        for kind in range(4):
            copy(ring, h, kind, 0).wait_send()

    each(0, 2, drain)


def kernel(
    dims,
    live_ref,
    lengths_ref,
    gain_ref,
    taps_ref,
    rates_ref,
    weight_ref,
    skip_ref,
    x_hbm,
    w_in_hbm,
    w_out_hbm,
    out_ref,
    comb,
    last_blocks,
    x_all,
    w_in,
    sums,
    squares,
    proj,
    query,
    gated,
    ends,
    starts,
    edge,
    mixed,
    g_all,
    out_sum,
    w_stage,
    w_half,
    w_mine,
    local_sems,
    shift_sems,
    split_sems,
    deep_sems,
    relay_sems,
    edge_sems,
    x_send,
    x_recv,
    g_send,
    g_recv,
):
    ctx_count, tokens, block, width = dims
    ctx = lax.axis_index("ctx")
    ch = lax.axis_index("ch")
    row = ch // SIDE
    col = lax.rem(ch, SIDE)
    partner = ctx + 1 - 2 * lax.rem(ctx, 2)
    depth_count = ctx_count // 2
    capacity = x_hbm.shape[0] // block
    own_blocks = tokens // block
    features = x_hbm.shape[1]
    part_rows = w_out_hbm.shape[0] // ctx_count
    half = tokens // 2
    modes = rates_ref.shape[0]
    tiles = rates_ref.shape[1] // LANES
    run = tokens // GROUPS

    x_in = pltpu.make_async_copy(x_hbm, comb.at[pl.ds(0, capacity * block)], local_sems.at[0])
    x_in.start()

    def w_part(other, target, sem):
        return pltpu.make_async_copy(
            w_out_hbm.at[
                pl.ds(pl.multiple_of(ctx * part_rows, part_rows), part_rows),
                pl.ds(pl.multiple_of(other * features, features), features),
            ],
            target,
            sem,
        )

    for x in range(SIDE):
        for y in range(SIDE):
            w_part(y * SIDE + x, w_stage.at[x, y], local_sems.at[2 + x * SIDE + y]).start()
    w_load = pltpu.make_async_copy(w_in_hbm, w_in, local_sems.at[1])
    w_load.start()

    barrier = pltpu.get_barrier_semaphore()
    for step in range(1, SIDE):
        pl.semaphore_signal(
            barrier, inc=1, device_id=(ctx, row * SIDE + lax.rem(col + step, SIDE)), device_id_type=MESH
        )
        pl.semaphore_signal(
            barrier, inc=1, device_id=(ctx, lax.rem(row + step, SIDE) * SIDE + col), device_id_type=MESH
        )
    for step in range(1, ctx_count):
        pl.semaphore_signal(
            barrier, inc=1, device_id=(lax.rem(ctx + step, ctx_count), ch), device_id_type=MESH
        )
    sums[...] = jnp.zeros_like(sums)
    squares[...] = jnp.zeros_like(squares)
    out_sum[...] = jnp.zeros_like(out_sum)
    x_in.wait()

    before = jnp.int32(0)
    for owner in range(ctx_count):
        before = before + jnp.where(owner < ctx, live_ref[owner], 0)
    here = live_ref[ctx]
    left_live = live_ref[lax.rem(ctx + ctx_count - 1, ctx_count)]
    first_sent = jnp.maximum(here - 2, 0)
    def pick(which, options):
        value = comb[pl.ds(options[0] * block, block), :]
        for option in options[1:]:
            value = jnp.where(which == option, comb[pl.ds(option * block, block), :], value)
        return value

    for i in range(2):
        last_blocks[pl.ds(i * block, block), :] = pick(first_sent + i, list(range(i, capacity - 1 + i)))
    pl.semaphore_wait(barrier, 2 * (SIDE - 1) + ctx_count - 1)

    after = lax.rem(ctx + 1, ctx_count)
    ahead = lax.rem(ctx + ctx_count - 1, ctx_count)
    to_next = remote(
        last_blocks,
        comb.at[pl.ds(capacity * block, 2 * block)],
        shift_sems.at[0],
        shift_sems.at[1],
        (after, ch),
    )
    to_previous = remote(
        comb.at[pl.ds(0, 2 * block)],
        comb.at[pl.ds((capacity + 2) * block, 2 * block)],
        shift_sems.at[2],
        shift_sems.at[3],
        (ahead, ch),
    )
    to_next.start()
    to_previous.start()

    for x in range(SIDE):
        for y in range(SIDE):
            w_part(y * SIDE + x, w_stage.at[x, y], local_sems.at[2 + x * SIDE + y]).wait()

    def along_x(step):
        x = lax.rem(col + step, SIDE)
        return remote(
            w_stage.at[x],
            w_half.at[col],
            split_sems.at[0, 0, step],
            split_sems.at[0, 1, step],
            (ctx, row * SIDE + x),
        )

    def along_y(step):
        y = lax.rem(row + step, SIDE)
        return remote(
            w_half.at[:, y],
            w_mine.at[ctx, pl.ds(row * SIDE, SIDE)],
            split_sems.at[1, 0, step],
            split_sems.at[1, 1, step],
            (ctx, y * SIDE + col),
        )

    def over_depth(step):
        return remote(
            w_mine.at[ctx],
            w_mine.at[ctx],
            deep_sems.at[0, step],
            deep_sems.at[1, step],
            (lax.rem(ctx + 2 * step, ctx_count), ch),
        )

    def to_partner(step):
        held = lax.rem(ctx + 2 * step, ctx_count)
        return remote(
            w_mine.at[held],
            w_mine.at[held],
            relay_sems.at[0, step],
            relay_sems.at[1, step],
            (partner, ch),
        )

    for step in range(1, SIDE):
        along_x(step).start()
    own_x = pltpu.make_async_copy(w_stage.at[col], w_half.at[col], local_sems.at[0])
    own_x.start()
    own_x.wait()

    to_next.wait_recv()
    to_previous.wait_recv()
    first_wanted = ctx * own_blocks
    for i in range(own_blocks):
        wanted = first_wanted + i
        back = before - wanted
        from_left = capacity + left_live - back - jnp.maximum(left_live - 2, 0)
        from_right = capacity + 2 + wanted - before - here
        source = jnp.where(wanted < before, from_left, jnp.where(wanted >= before + here, from_right, wanted - before))
        nearby = list(range(max(i - 2, 0), min(i + 3, capacity))) + list(range(capacity, capacity + 4))
        x_all[ch, (2 * i) // own_blocks, pl.ds((i * block) % half, block), :] = pick(source, nearby)

    def project(h, g):
        wide = x_all[g, h].astype(jnp.float32)
        squared = wide * wide
        folded = squared[:, :LANES]
        for lane in range(1, features // LANES):
            folded = folded + squared[:, lane * LANES : (lane + 1) * LANES]
        at = pl.ds(pl.multiple_of(h * half, half), half)
        squares[at, :] = squares[at, :] + folded
        scaled = (wide * gain_ref[pl.ds(g, 1), :]).astype(jnp.bfloat16)
        deep = pl.ds(pl.multiple_of(g * features, features), features)
        for branch in range(BRANCHES):
            sums[branch, at, :] = sums[branch, at, :] + jnp.dot(
                scaled, w_in[branch, deep, :], preferred_element_type=jnp.float32
            )

    w_load.wait()
    for step in range(1, SIDE):
        along_x(step).wait_recv()
    for step in range(1, SIDE):
        along_y(step).start()
    own_y = pltpu.make_async_copy(w_half.at[:, row], w_mine.at[ctx, pl.ds(row * SIDE, SIDE)], local_sems.at[0])
    own_y.start()
    own_y.wait()
    for step in range(1, SIDE):
        along_y(step).wait_recv()
    for step in range(1, depth_count):
        over_depth(step).start()
    to_partner(0).start()
    plane_gather(x_all, x_send, x_recv, ctx, row, col, project)
    for step in range(1, depth_count):
        over_depth(depth_count - step).wait_recv()
        to_partner(step).start()

    def scale_rows(begin, count):
        total = jnp.sum(squares[pl.ds(begin, count), :], axis=1, keepdims=True)
        scale = lax.rsqrt(total / width + EPS)
        for branch in range(BRANCHES):
            for tile in range(tiles):
                proj[branch, tile, pl.ds(begin + 8, count), :] = (
                    sums[branch, pl.ds(begin, count), tile * LANES : (tile + 1) * LANES] * scale
                )

    scale_rows(tokens - run, run)
    halo = remote(
        proj.at[:, :, pl.ds(tokens, 8)],
        proj.at[:, :, pl.ds(0, 8)],
        shift_sems.at[4],
        shift_sems.at[5],
        (after, ch),
    )
    halo.start()
    each(0, GROUPS - 1, lambda i: scale_rows(pl.multiple_of(i * run, run), run))
    halo.wait_recv()

    cut_one = lengths_ref[0]
    cut_two = cut_one + lengths_ref[1]
    base = ctx * tokens
    group_start = base + run * lax.broadcasted_iota(jnp.int32, (GROUPS, LANES), 0)

    def keep_at(t):
        token = group_start + t
        begins = (token == 0) | (token == cut_one) | (token == cut_two)
        return jnp.where(begins, 0.0, 1.0).astype(jnp.float32)

    def unbroken(begin, count):
        cut = (begin == 0) | ((cut_one >= begin) & (cut_one < begin + count)) | ((cut_two >= begin) & (cut_two < begin + count))
        return jnp.where(cut, 0.0, 1.0).astype(jnp.float32)

    def spread_row(values):
        return jnp.broadcast_to(values, (GROUPS, LANES))

    for tile in range(tiles):
        lanes = pl.ds(tile * LANES, LANES)
        decays = [spread_row(jnp.exp(-rates_ref[pl.ds(m, 1), lanes])) for m in range(modes)]
        taps = [
            [spread_row(taps_ref[tap, pl.ds(branch, 1), lanes]) for branch in range(BRANCHES)]
            for tap in range(TAPS)
        ]

        def collect(t, carry, tile=tile, decays=decays, taps=taps):
            states, one_back, two_back, keep_before = carry
            keep = keep_at(t)
            far = keep * keep_before
            now = [proj[branch, tile, pl.ds(8 + t, GROUPS, stride=run), :] for branch in range(BRANCHES)]
            parts = [
                taps[0][branch] * now[branch]
                + taps[1][branch] * (keep * one_back[branch])
                + taps[2][branch] * (far * two_back[branch])
                for branch in range(BRANCHES)
            ]
            entered = parts[1] * parts[2]
            query[tile, t] = parts[0]
            gated[tile, t] = entered
            states = [decays[m] * (states[m] * keep) + entered for m in range(modes)]
            return (states, now, one_back, keep)

        first = [proj[branch, tile, pl.ds(7, GROUPS, stride=run), :] for branch in range(BRANCHES)]
        second = [proj[branch, tile, pl.ds(6, GROUPS, stride=run), :] for branch in range(BRANCHES)]
        zero = jnp.zeros((GROUPS, LANES), jnp.float32)
        done = lax.fori_loop(0, run, collect, ([zero] * modes, first, second, keep_at(-1)))
        for m in range(modes):
            ends[tile, pl.ds(m * GROUPS, GROUPS), :] = done[0][m]

    run_decay = [jnp.exp(-run * rates_ref[:, pl.ds(tile * LANES, LANES)]) for tile in range(tiles)]
    all_decay = [jnp.exp(-tokens * rates_ref[:, pl.ds(tile * LANES, LANES)]) for tile in range(tiles)]
    unbroken_run = [unbroken(base + run * i, run) for i in range(GROUPS)]

    for tile in range(tiles):
        state = jnp.zeros((modes, LANES), jnp.float32)
        for i in range(GROUPS):
            state = ends[tile, pl.ds(i, modes, stride=GROUPS), :] + (unbroken_run[i] * run_decay[tile]) * state
        edge[ctx, tile] = state

    def edge_to(step):
        return remote(
            edge.at[ctx],
            edge.at[ctx],
            edge_sems.at[0, step],
            edge_sems.at[1, step],
            (lax.rem(ctx + step, ctx_count), ch),
        )

    for step in range(1, ctx_count):
        edge_to(step).start()
    for step in range(1, ctx_count):
        edge_to(step).wait_recv()

    for tile in range(tiles):
        state = jnp.zeros((modes, LANES), jnp.float32)
        for device in range(ctx_count):
            moved = edge[device, tile] + (unbroken(jnp.int32(device * tokens), tokens) * all_decay[tile]) * state
            state = jnp.where(device < ctx, moved, state)
        for i in range(GROUPS):
            starts[tile, pl.ds(i, modes, stride=GROUPS), :] = state
            if i < GROUPS - 1:
                state = ends[tile, pl.ds(i, modes, stride=GROUPS), :] + (unbroken_run[i] * run_decay[tile]) * state

    for tile in range(tiles):
        lanes = pl.ds(tile * LANES, LANES)
        decays = [spread_row(jnp.exp(-rates_ref[pl.ds(m, 1), lanes])) for m in range(modes)]
        weights = [spread_row(weight_ref[pl.ds(m, 1), lanes]) for m in range(modes)]
        direct = spread_row(skip_ref[:, lanes])

        def filtered(t, states, tile=tile, decays=decays, weights=weights, direct=direct):
            keep = keep_at(t)
            entered = gated[tile, t]
            states = [decays[m] * (states[m] * keep) + entered for m in range(modes)]
            terms = [weights[m] * states[m] for m in range(modes)] + [direct * entered]
            while len(terms) > 1:
                terms = [
                    terms[k] + terms[k + 1] if k + 1 < len(terms) else terms[k]
                    for k in range(0, len(terms), 2)
                ]
            mixed[tile, pl.ds(t, GROUPS, stride=run), :] = query[tile, t] * terms[0]
            return states

        lax.fori_loop(
            0, run, filtered, [starts[tile, pl.ds(m * GROUPS, GROUPS), :] for m in range(modes)]
        )
        for h in range(2):
            g_all[ch, h, :, lanes] = mixed[tile, pl.ds(h * half, half), :].astype(jnp.bfloat16)

    for step in range(1, depth_count):
        to_partner(depth_count - step).wait_recv()
    to_partner(0).wait_recv()

    def multiply_out(h, g):
        weights = w_mine[:, g].reshape(ctx_count * part_rows, features)
        out_sum[h] = out_sum[h] + jnp.dot(g_all[g, h], weights, preferred_element_type=jnp.float32)

    plane_gather(g_all, g_send, g_recv, ctx, row, col, multiply_out)
    for h in range(2):
        out_ref[:, pl.ds(h * half, half)] = jnp.transpose(out_sum[h]).astype(jnp.bfloat16)

    to_next.wait_send()
    to_previous.wait_send()
    halo.wait_send()
    for step in range(1, SIDE):
        along_x(step).wait_send()
        along_y(step).wait_send()
    for step in range(1, depth_count):
        over_depth(step).wait_send()
    for step in range(depth_count):
        to_partner(step).wait_send()
    for step in range(1, ctx_count):
        edge_to(step).wait_send()


def body(
    x_owned,
    live_blocks,
    seq_lengths,
    norm_gain,
    w_in,
    w_short,
    decay_rates,
    residues,
    skip_gain,
    w_out,
):
    ctx_count = lax.axis_size("ctx")
    ch_count = lax.axis_size("ch")
    width = norm_gain.shape[0]
    features = x_owned.shape[1]
    tokens = x_owned.shape[0] // 2
    block = tokens // 4
    half = tokens // 2
    run = tokens // GROUPS
    modes, channels = decay_rates.shape
    tiles = channels // LANES
    part_rows = channels // ctx_count
    mode_weight = residues * jnp.sqrt(-jnp.expm1(-2.0 * decay_rates))
    bf16, f32 = jnp.bfloat16, jnp.float32
    smem = pl.BlockSpec(memory_space=pltpu.SMEM)
    vmem = pl.BlockSpec(memory_space=pltpu.VMEM)
    anywhere = pl.BlockSpec(memory_space=pl.ANY)
    dma = pltpu.SemaphoreType.DMA
    flops = 2 * tokens * width * BRANCHES * channels + 2 * tokens * features * ch_count * channels
    return pl.pallas_call(
        functools.partial(kernel, (ctx_count, tokens, block, width)),
        out_shape=jax.ShapeDtypeStruct((features, tokens), bf16),
        in_specs=[smem, smem, vmem, vmem, vmem, vmem, vmem, anywhere, anywhere, anywhere],
        out_specs=vmem,
        scratch_shapes=[
            pltpu.VMEM((x_owned.shape[0] + 4 * block, features), bf16),
            pltpu.VMEM((2 * block, features), bf16),
            pltpu.VMEM((ch_count, 2, half, features), bf16),
            pltpu.VMEM((BRANCHES, width, channels), bf16),
            pltpu.VMEM((BRANCHES, tokens, channels), f32),
            pltpu.VMEM((tokens, LANES), f32),
            pltpu.VMEM((BRANCHES, tiles, tokens + 8, LANES), f32),
            pltpu.VMEM((tiles, run, GROUPS, LANES), f32),
            pltpu.VMEM((tiles, run, GROUPS, LANES), f32),
            pltpu.VMEM((tiles, modes * GROUPS, LANES), f32),
            pltpu.VMEM((tiles, modes * GROUPS, LANES), f32),
            pltpu.VMEM((ctx_count, tiles, modes, LANES), f32),
            pltpu.VMEM((tiles, tokens, LANES), f32),
            pltpu.VMEM((ch_count, 2, half, channels), bf16),
            pltpu.VMEM((2, half, features), f32),
            pltpu.VMEM((SIDE, SIDE, part_rows, features), bf16),
            pltpu.VMEM((SIDE, SIDE, part_rows, features), bf16),
            pltpu.VMEM((ctx_count, ch_count, part_rows, features), bf16),
            dma((2 + ch_count,)),
            dma((6,)),
            dma((2, 2, SIDE)),
            dma((2, ctx_count // 2)),
            dma((2, ctx_count // 2)),
            dma((2, ctx_count)),
            dma((SIDE + 1, 2, 4)),
            dma((SIDE + 1, 2, 4)),
            dma((SIDE + 1, 2, 4)),
            dma((SIDE + 1, 2, 4)),
        ],
        compiler_params=pltpu.CompilerParams(
            collective_id=0, has_side_effects=True, vmem_limit_bytes=56 * 1024 * 1024
        ),
        cost_estimate=pl.CostEstimate(flops=flops, bytes_accessed=18 << 20, transcendentals=0),
    )(
        live_blocks,
        seq_lengths,
        norm_gain.reshape(ch_count, features),
        w_short,
        decay_rates,
        mode_weight,
        skip_gain.reshape(1, channels),
        x_owned,
        w_in,
        w_out,
    )


def solution(mesh):
    return jax.shard_map(
        body,
        mesh=mesh,
        in_specs=(
            P("ctx", "ch"),
            P(),
            P(),
            P(),
            P(None, None, "ch"),
            P(None, None, "ch"),
            P(None, "ch"),
            P(None, "ch"),
            P("ch"),
            P("ch", None),
        ),
        out_specs=P("ch", "ctx"),
        check_vma=False,
    )
```

```python
import functools

import jax
import jax.numpy as jnp
from jax import lax
from jax.experimental import pallas as pl
from jax.experimental.pallas import tpu as pltpu
from jax.sharding import PartitionSpec as P

EPS = 1e-06
TAPS = 3
BRANCHES = 3
SIDE = 4
LANES = 128
GROUPS = 8
MESH = pl.DeviceIdType.MESH


def remote(src, dst, send_sem, recv_sem, device):
    return pltpu.make_async_remote_copy(
        src_ref=src,
        dst_ref=dst,
        send_sem=send_sem,
        recv_sem=recv_sem,
        device_id=device,
        device_id_type=MESH,
    )


def each(lower, upper, step):
    def run(index, carry):
        step(index)
        return carry

    lax.fori_loop(lower, upper, run, 0)


def plane_gather(buf, send_sems, recv_sems, ctx, row, col, use):
    half = buf.shape[2]
    quarter = half // 2
    rows = (pl.ds(0, half), pl.ds(0, half), pl.ds(0, quarter), pl.ds(quarter, quarter))

    def place(h, first, second):
        x = lax.rem(col + (1 - h) * first + h * second + 2 * SIDE, SIDE)
        y = lax.rem(row + (1 - h) * second + h * first + 2 * SIDE, SIDE)
        return y * SIDE + x

    def offset(ring):
        k = ring - 1
        return k + k // 2 - 2 * (k // 3)

    def piece(ring, h, along):
        if isinstance(ring, int) and ring == 0:
            return place(h, along, 0)
        return place(h, offset(ring), along)

    def neighbour(ring, h, along):
        if isinstance(ring, int) and ring == 0:
            return (ctx, place(h, along, 0))
        return (ctx, place(h, 0, along))

    def copy(ring, h, kind, along):
        part = buf.at[piece(ring, h, along), h, rows[kind]]
        return remote(
            part,
            part,
            send_sems.at[ring, h, kind],
            recv_sems.at[ring, h, kind],
            neighbour(ring, h, 1 - 2 * (kind % 2)),
        )

    def send(ring, h):
        copy(ring, h, 0, 0).start()
        copy(ring, h, 1, 0).start()

    def forward(ring, h):
        copy(ring, h, 0, -1).wait_recv()
        copy(ring, h, 2, -1).start()
        copy(ring, h, 1, 1).wait_recv()
        copy(ring, h, 3, 1).start()

    def finish(ring, h):
        copy(ring, h, 2, 2).wait_recv()
        copy(ring, h, 3, 2).wait_recv()

    def open_rings(h):
        send(0, h)
        send(1, h)

    def grow(h):
        forward(0, h)
        send(2, h)
        send(3, h)

    def close_first(h):
        finish(0, h)
        send(4, h)

    def rest(opened, grown):
        opened()
        each(0, 2, lambda h: use(h, place(h, 0, 0)))
        each(0, 2, grow)
        grown()
        each(0, 4, lambda i: use(i // 2, piece(0, i // 2, 2 * (i % 2) - 1)))
        each(0, 2, close_first)
        each(0, 2, lambda h: use(h, piece(0, h, 2)))
        each(1, SIDE + 1, pass_on)
        each(1, SIDE + 1, take_last)
        each(0, 2, drain)

    def pass_on(ring):
        each(0, 2, lambda h: forward(ring, h))
        each(0, 4, lambda i: use(i // 2, piece(ring, i // 2, 2 * (i % 2) - 1)))

    def take_last(ring):
        each(0, 2, lambda h: finish(ring, h))
        each(0, 2, lambda h: use(h, piece(ring, h, 2)))

    def drain(index):
        h = index % 2
        for kind in range(4):
            copy(0, h, kind, 0).wait_send()
        each(1, SIDE + 1, lambda ring: drain_ring(ring, h))

    def drain_ring(ring, h):
        for kind in range(4):
            copy(ring, h, kind, 0).wait_send()

    return open_rings, rest


def kernel(
    dims,
    live_ref,
    lengths_ref,
    gain_ref,
    taps_ref,
    rates_ref,
    weight_ref,
    skip_ref,
    x_hbm,
    w_in_hbm,
    w_out_hbm,
    out_ref,
    comb,
    last_blocks,
    x_all,
    w_in,
    sums,
    squares,
    proj,
    query,
    gated,
    ends,
    starts,
    edge,
    mixed,
    g_all,
    out_sum,
    w_stage,
    w_half,
    w_mine,
    local_sems,
    shift_sems,
    split_sems,
    deep_sems,
    relay_sems,
    edge_sems,
    x_send,
    x_recv,
    g_send,
    g_recv,
):
    ctx_count, tokens, block, width = dims
    ctx = lax.axis_index("ctx")
    ch = lax.axis_index("ch")
    row = ch // SIDE
    col = lax.rem(ch, SIDE)
    partner = ctx + 1 - 2 * lax.rem(ctx, 2)
    depth_count = ctx_count // 2
    capacity = x_hbm.shape[0] // block
    own_blocks = tokens // block
    features = x_hbm.shape[1]
    part_rows = w_out_hbm.shape[0] // ctx_count
    half = tokens // 2
    modes = rates_ref.shape[0]
    tiles = rates_ref.shape[1] // LANES
    run = tokens // GROUPS

    x_in = pltpu.make_async_copy(x_hbm, comb.at[pl.ds(0, capacity * block)], local_sems.at[0])
    x_in.start()

    def w_part(other, target, sem):
        return pltpu.make_async_copy(
            w_out_hbm.at[
                pl.ds(pl.multiple_of(ctx * part_rows, part_rows), part_rows),
                pl.ds(pl.multiple_of(other * features, features), features),
            ],
            target,
            sem,
        )

    for x in range(SIDE):
        for y in range(SIDE):
            w_part(y * SIDE + x, w_stage.at[x, y], local_sems.at[2 + x * SIDE + y]).start()
    w_load = pltpu.make_async_copy(w_in_hbm, w_in, local_sems.at[1])
    w_load.start()

    barrier = pltpu.get_barrier_semaphore()
    for step in range(1, SIDE):
        pl.semaphore_signal(
            barrier, inc=1, device_id=(ctx, row * SIDE + lax.rem(col + step, SIDE)), device_id_type=MESH
        )
        pl.semaphore_signal(
            barrier, inc=1, device_id=(ctx, lax.rem(row + step, SIDE) * SIDE + col), device_id_type=MESH
        )
    for step in range(1, ctx_count):
        pl.semaphore_signal(
            barrier, inc=1, device_id=(lax.rem(ctx + step, ctx_count), ch), device_id_type=MESH
        )
    sums[...] = jnp.zeros_like(sums)
    squares[...] = jnp.zeros_like(squares)
    out_sum[...] = jnp.zeros_like(out_sum)
    x_in.wait()

    before = jnp.int32(0)
    for owner in range(ctx_count):
        before = before + jnp.where(owner < ctx, live_ref[owner], 0)
    here = live_ref[ctx]
    left_live = live_ref[lax.rem(ctx + ctx_count - 1, ctx_count)]
    first_sent = jnp.maximum(here - 2, 0)
    def pick(which, options):
        value = comb[pl.ds(options[0] * block, block), :]
        for option in options[1:]:
            value = jnp.where(which == option, comb[pl.ds(option * block, block), :], value)
        return value

    for i in range(2):
        last_blocks[pl.ds(i * block, block), :] = pick(first_sent + i, list(range(i, capacity - 1 + i)))
    pl.semaphore_wait(barrier, 2 * (SIDE - 1) + ctx_count - 1)

    after = lax.rem(ctx + 1, ctx_count)
    ahead = lax.rem(ctx + ctx_count - 1, ctx_count)
    to_next = remote(
        last_blocks,
        comb.at[pl.ds(capacity * block, 2 * block)],
        shift_sems.at[0],
        shift_sems.at[1],
        (after, ch),
    )
    to_previous = remote(
        comb.at[pl.ds(0, 2 * block)],
        comb.at[pl.ds((capacity + 2) * block, 2 * block)],
        shift_sems.at[2],
        shift_sems.at[3],
        (ahead, ch),
    )
    to_next.start()
    to_previous.start()

    for x in range(SIDE):
        for y in range(SIDE):
            w_part(y * SIDE + x, w_stage.at[x, y], local_sems.at[2 + x * SIDE + y]).wait()

    def along_x(step):
        x = lax.rem(col + step, SIDE)
        return remote(
            w_stage.at[x],
            w_half.at[col],
            split_sems.at[0, 0, step],
            split_sems.at[0, 1, step],
            (ctx, row * SIDE + x),
        )

    def along_y(step):
        y = lax.rem(row + step, SIDE)
        return remote(
            w_half.at[:, y],
            w_mine.at[ctx, pl.ds(row * SIDE, SIDE)],
            split_sems.at[1, 0, step],
            split_sems.at[1, 1, step],
            (ctx, y * SIDE + col),
        )

    def over_depth(step):
        return remote(
            w_mine.at[ctx],
            w_mine.at[ctx],
            deep_sems.at[0, step],
            deep_sems.at[1, step],
            (lax.rem(ctx + 2 * step, ctx_count), ch),
        )

    def to_partner(step):
        held = lax.rem(ctx + 2 * step, ctx_count)
        return remote(
            w_mine.at[held],
            w_mine.at[held],
            relay_sems.at[0, step],
            relay_sems.at[1, step],
            (partner, ch),
        )

    for step in range(1, SIDE):
        along_x(step).start()
    own_x = pltpu.make_async_copy(w_stage.at[col], w_half.at[col], local_sems.at[0])
    own_x.start()
    own_x.wait()

    def fill(h):
        for i in range(h * own_blocks // 2, (h + 1) * own_blocks // 2):
            wanted = ctx * own_blocks + i
            local = list(range(max(i - 2, 0), min(i + 3, capacity)))
            if h == 0:
                other = capacity + left_live - (before - wanted) - jnp.maximum(left_live - 2, 0)
                source = jnp.where(wanted < before, other, wanted - before)
                options = local + [capacity, capacity + 1]
            else:
                other = capacity + 2 + wanted - before - here
                source = jnp.where(wanted >= before + here, other, wanted - before)
                options = local + [capacity + 2, capacity + 3]
            x_all[ch, h, pl.ds((i * block) % half, block), :] = pick(source, options)

    def project(h, g):
        wide = x_all[g, h].astype(jnp.float32)
        squared = wide * wide
        folded = squared[:, :LANES]
        for lane in range(1, features // LANES):
            folded = folded + squared[:, lane * LANES : (lane + 1) * LANES]
        at = pl.ds(pl.multiple_of(h * half, half), half)
        squares[at, :] = squares[at, :] + folded
        deep = pl.ds(pl.multiple_of(g * features, features), features)
        scaled = (wide * gain_ref[:, deep]).astype(jnp.bfloat16)
        for branch in range(BRANCHES):
            sums[branch, at, :] = sums[branch, at, :] + jnp.dot(
                scaled, w_in[branch, deep, :], preferred_element_type=jnp.float32
            )

    def second_leg():
        for step in range(1, SIDE):
            along_x(step).wait_recv()
        for step in range(1, SIDE):
            along_y(step).start()
        own_y.start()
        w_load.wait()

    def third_leg():
        for step in range(1, SIDE):
            along_y(step).wait_recv()
        own_y.wait()
        for step in range(1, depth_count):
            over_depth(step).start()
        to_partner(0).start()

    own_y = pltpu.make_async_copy(w_half.at[:, row], w_mine.at[ctx, pl.ds(row * SIDE, SIDE)], local_sems.at[0])
    open_x, rest_x = plane_gather(x_all, x_send, x_recv, ctx, row, col, project)
    parity = lax.rem(ctx, 2)

    def take(h):
        @pl.when(h == 0)
        def _():
            to_next.wait_recv()
            fill(0)

        @pl.when(h == 1)
        def _():
            to_previous.wait_recv()
            fill(1)

        open_x(h)

    take(1 - parity)
    take(parity)
    rest_x(second_leg, third_leg)
    def scale_rows(begin, count):
        total = jnp.sum(squares[pl.ds(begin, count), :], axis=1, keepdims=True)
        scale = lax.rsqrt(total / width + EPS)
        for branch in range(BRANCHES):
            for tile in range(tiles):
                proj[branch, tile, pl.ds(begin + 8, count), :] = (
                    sums[branch, pl.ds(begin, count), tile * LANES : (tile + 1) * LANES] * scale
                )

    scale_rows(tokens - run, run)
    halo = remote(
        proj.at[:, :, pl.ds(tokens, 8)],
        proj.at[:, :, pl.ds(0, 8)],
        shift_sems.at[4],
        shift_sems.at[5],
        (after, ch),
    )
    halo.start()
    each(0, GROUPS - 1, lambda i: scale_rows(pl.multiple_of(i * run, run), run))
    halo.wait_recv()

    cut_one = lengths_ref[0]
    cut_two = cut_one + lengths_ref[1]
    base = ctx * tokens
    group_start = base + run * lax.broadcasted_iota(jnp.int32, (GROUPS, LANES), 0)

    def keep_at(t):
        token = group_start + t
        begins = (token == 0) | (token == cut_one) | (token == cut_two)
        return jnp.where(begins, 0.0, 1.0).astype(jnp.float32)

    def unbroken(begin, count):
        cut = (begin == 0) | ((cut_one >= begin) & (cut_one < begin + count)) | ((cut_two >= begin) & (cut_two < begin + count))
        return jnp.where(cut, 0.0, 1.0).astype(jnp.float32)

    def spread_row(values):
        return jnp.broadcast_to(values, (GROUPS, LANES))

    for tile in range(tiles):
        lanes = pl.ds(tile * LANES, LANES)
        decays = [spread_row(jnp.exp(-rates_ref[pl.ds(m, 1), lanes])) for m in range(modes)]
        taps = [
            [spread_row(taps_ref[tap, pl.ds(branch, 1), lanes]) for branch in range(BRANCHES)]
            for tap in range(TAPS)
        ]

        def collect(t, carry, tile=tile, decays=decays, taps=taps):
            states, one_back, two_back, keep_before = carry
            keep = keep_at(t)
            far = keep * keep_before
            now = [proj[branch, tile, pl.ds(8 + t, GROUPS, stride=run), :] for branch in range(BRANCHES)]
            parts = [
                taps[0][branch] * now[branch]
                + taps[1][branch] * (keep * one_back[branch])
                + taps[2][branch] * (far * two_back[branch])
                for branch in range(BRANCHES)
            ]
            entered = parts[1] * parts[2]
            query[tile, t] = parts[0]
            gated[tile, t] = entered
            states = [decays[m] * (states[m] * keep) + entered for m in range(modes)]
            return (states, now, one_back, keep)

        first = [proj[branch, tile, pl.ds(7, GROUPS, stride=run), :] for branch in range(BRANCHES)]
        second = [proj[branch, tile, pl.ds(6, GROUPS, stride=run), :] for branch in range(BRANCHES)]
        zero = jnp.zeros((GROUPS, LANES), jnp.float32)
        done = lax.fori_loop(0, run, collect, ([zero] * modes, first, second, keep_at(-1)), unroll=4)
        for m in range(modes):
            ends[tile, pl.ds(m * GROUPS, GROUPS), :] = done[0][m]

    run_decay = [jnp.exp(-run * rates_ref[:, pl.ds(tile * LANES, LANES)]) for tile in range(tiles)]
    all_decay = [jnp.exp(-tokens * rates_ref[:, pl.ds(tile * LANES, LANES)]) for tile in range(tiles)]
    unbroken_run = [unbroken(base + run * i, run) for i in range(GROUPS)]

    for tile in range(tiles):
        state = jnp.zeros((modes, LANES), jnp.float32)
        for i in range(GROUPS):
            state = ends[tile, pl.ds(i, modes, stride=GROUPS), :] + (unbroken_run[i] * run_decay[tile]) * state
        edge[ctx, tile] = state

    def edge_to(step):
        return remote(
            edge.at[ctx],
            edge.at[ctx],
            edge_sems.at[0, step],
            edge_sems.at[1, step],
            (lax.rem(ctx + step, ctx_count), ch),
        )

    for step in range(1, ctx_count):
        edge_to(step).start()
    for step in range(1, depth_count):
        over_depth(depth_count - step).wait_recv()
        to_partner(step).start()
    for step in range(1, ctx_count):
        edge_to(step).wait_recv()

    for tile in range(tiles):
        state = jnp.zeros((modes, LANES), jnp.float32)
        for device in range(ctx_count):
            moved = edge[device, tile] + (unbroken(jnp.int32(device * tokens), tokens) * all_decay[tile]) * state
            state = jnp.where(device < ctx, moved, state)
        for i in range(GROUPS):
            starts[tile, pl.ds(i, modes, stride=GROUPS), :] = state
            if i < GROUPS - 1:
                state = ends[tile, pl.ds(i, modes, stride=GROUPS), :] + (unbroken_run[i] * run_decay[tile]) * state

    def multiply_out(h, g):
        parts = LANES // part_rows
        weights = w_mine[pl.ds(h * parts, parts), g].reshape(LANES, features)
        out_sum[...] = out_sum[...] + jnp.dot(g_all[g, h], weights, preferred_element_type=jnp.float32)

    open_g, rest_g = plane_gather(g_all, g_send, g_recv, ctx, row, col, multiply_out)

    for tile in range(tiles):
        lanes = pl.ds(tile * LANES, LANES)
        decays = [spread_row(jnp.exp(-rates_ref[pl.ds(m, 1), lanes])) for m in range(modes)]
        weights = [spread_row(weight_ref[pl.ds(m, 1), lanes]) for m in range(modes)]
        direct = spread_row(skip_ref[:, lanes])

        def filtered(t, states, tile=tile, decays=decays, weights=weights, direct=direct):
            keep = keep_at(t)
            entered = gated[tile, t]
            states = [decays[m] * (states[m] * keep) + entered for m in range(modes)]
            terms = [weights[m] * states[m] for m in range(modes)] + [direct * entered]
            while len(terms) > 1:
                terms = [
                    terms[k] + terms[k + 1] if k + 1 < len(terms) else terms[k]
                    for k in range(0, len(terms), 2)
                ]
            mixed[tile, pl.ds(t, GROUPS, stride=run), :] = query[tile, t] * terms[0]
            return states

        lax.fori_loop(
            0, run, filtered, [starts[tile, pl.ds(m * GROUPS, GROUPS), :] for m in range(modes)], unroll=4
        )
        g_all[ch, tile] = mixed[tile].astype(jnp.bfloat16)
        open_g(tile)

    def last_leg():
        for step in range(1, depth_count):
            to_partner(depth_count - step).wait_recv()
        to_partner(0).wait_recv()

    rest_g(last_leg, lambda: None)
    for h in range(2):
        out_ref[:, pl.ds(h * half, half)] = jnp.transpose(out_sum[pl.ds(h * half, half), :]).astype(jnp.bfloat16)

    to_next.wait_send()
    to_previous.wait_send()
    halo.wait_send()
    for step in range(1, SIDE):
        along_x(step).wait_send()
        along_y(step).wait_send()
    for step in range(1, depth_count):
        over_depth(step).wait_send()
    for step in range(depth_count):
        to_partner(step).wait_send()
    for step in range(1, ctx_count):
        edge_to(step).wait_send()


def body(
    x_owned,
    live_blocks,
    seq_lengths,
    norm_gain,
    w_in,
    w_short,
    decay_rates,
    residues,
    skip_gain,
    w_out,
):
    ctx_count = lax.axis_size("ctx")
    ch_count = lax.axis_size("ch")
    width = norm_gain.shape[0]
    features = x_owned.shape[1]
    tokens = x_owned.shape[0] // 2
    block = tokens // 4
    half = tokens // 2
    run = tokens // GROUPS
    modes, channels = decay_rates.shape
    tiles = channels // LANES
    part_rows = channels // ctx_count
    mode_weight = residues * jnp.sqrt(-jnp.expm1(-2.0 * decay_rates))
    bf16, f32 = jnp.bfloat16, jnp.float32
    smem = pl.BlockSpec(memory_space=pltpu.SMEM)
    vmem = pl.BlockSpec(memory_space=pltpu.VMEM)
    anywhere = pl.BlockSpec(memory_space=pl.ANY)
    dma = pltpu.SemaphoreType.DMA
    flops = 2 * tokens * width * BRANCHES * channels + 2 * tokens * features * ch_count * channels
    return pl.pallas_call(
        functools.partial(kernel, (ctx_count, tokens, block, width)),
        out_shape=jax.ShapeDtypeStruct((features, tokens), bf16),
        in_specs=[smem, smem, vmem, vmem, vmem, vmem, vmem, anywhere, anywhere, anywhere],
        out_specs=vmem,
        scratch_shapes=[
            pltpu.VMEM((x_owned.shape[0] + 4 * block, features), bf16),
            pltpu.VMEM((2 * block, features), bf16),
            pltpu.VMEM((ch_count, 2, half, features), bf16),
            pltpu.VMEM((BRANCHES, width, channels), bf16),
            pltpu.VMEM((BRANCHES, tokens, channels), f32),
            pltpu.VMEM((tokens, LANES), f32),
            pltpu.VMEM((BRANCHES, tiles, tokens + 8, LANES), f32),
            pltpu.VMEM((tiles, run, GROUPS, LANES), f32),
            pltpu.VMEM((tiles, run, GROUPS, LANES), f32),
            pltpu.VMEM((tiles, modes * GROUPS, LANES), f32),
            pltpu.VMEM((tiles, modes * GROUPS, LANES), f32),
            pltpu.VMEM((ctx_count, tiles, modes, LANES), f32),
            pltpu.VMEM((tiles, tokens, LANES), f32),
            pltpu.VMEM((ch_count, tiles, tokens, LANES), bf16),
            pltpu.VMEM((tokens, features), f32),
            pltpu.VMEM((SIDE, SIDE, part_rows, features), bf16),
            pltpu.VMEM((SIDE, SIDE, part_rows, features), bf16),
            pltpu.VMEM((ctx_count, ch_count, part_rows, features), bf16),
            dma((2 + ch_count,)),
            dma((6,)),
            dma((2, 2, SIDE)),
            dma((2, ctx_count // 2)),
            dma((2, ctx_count // 2)),
            dma((2, ctx_count)),
            dma((SIDE + 1, 2, 4)),
            dma((SIDE + 1, 2, 4)),
            dma((SIDE + 1, 2, 4)),
            dma((SIDE + 1, 2, 4)),
        ],
        compiler_params=pltpu.CompilerParams(
            collective_id=0, has_side_effects=True, vmem_limit_bytes=56 * 1024 * 1024
        ),
        cost_estimate=pl.CostEstimate(flops=flops, bytes_accessed=18 << 20, transcendentals=0),
    )(
        live_blocks,
        seq_lengths,
        norm_gain.reshape(1, width),
        w_short,
        decay_rates,
        mode_weight,
        skip_gain.reshape(1, channels),
        x_owned,
        w_in,
        w_out,
    )


def solution(mesh):
    return jax.shard_map(
        body,
        mesh=mesh,
        in_specs=(
            P("ctx", "ch"),
            P(),
            P(),
            P(),
            P(None, None, "ch"),
            P(None, None, "ch"),
            P(None, "ch"),
            P(None, "ch"),
            P("ch"),
            P("ch", None),
        ),
        out_specs=P("ch", "ctx"),
        check_vma=False,
    )
```

```python
import functools

import jax
import jax.numpy as jnp
from jax import lax
from jax.experimental import pallas as pl
from jax.experimental.pallas import tpu as pltpu
from jax.sharding import PartitionSpec as P

EPS = 1e-06
TAPS = 3
BRANCHES = 3
SIDE = 4
LANES = 128
GROUPS = 8
MESH = pl.DeviceIdType.MESH


def remote(src, dst, send_sem, recv_sem, device):
    return pltpu.make_async_remote_copy(
        src_ref=src,
        dst_ref=dst,
        send_sem=send_sem,
        recv_sem=recv_sem,
        device_id=device,
        device_id_type=MESH,
    )


def each(lower, upper, step):
    def run(index, carry):
        step(index)
        return carry

    lax.fori_loop(lower, upper, run, 0)


def plane_gather(buf, send_sems, recv_sems, ctx, row, col, use):
    half = buf.shape[2]
    quarter = half // 2
    rows = (pl.ds(0, half), pl.ds(0, half), pl.ds(0, quarter), pl.ds(quarter, quarter))

    def place(h, first, second):
        x = lax.rem(col + (1 - h) * first + h * second + 2 * SIDE, SIDE)
        y = lax.rem(row + (1 - h) * second + h * first + 2 * SIDE, SIDE)
        return y * SIDE + x

    def offset(ring):
        k = ring - 1
        return k + k // 2 - 2 * (k // 3)

    def piece(ring, h, along):
        if isinstance(ring, int) and ring == 0:
            return place(h, along, 0)
        return place(h, offset(ring), along)

    def neighbour(ring, h, along):
        if isinstance(ring, int) and ring == 0:
            return (ctx, place(h, along, 0))
        return (ctx, place(h, 0, along))

    def copy(ring, h, kind, along):
        part = buf.at[piece(ring, h, along), h, rows[kind]]
        return remote(
            part,
            part,
            send_sems.at[ring, h, kind],
            recv_sems.at[ring, h, kind],
            neighbour(ring, h, 1 - 2 * (kind % 2)),
        )

    def send(ring, h):
        copy(ring, h, 0, 0).start()
        copy(ring, h, 1, 0).start()

    def forward(ring, h):
        copy(ring, h, 0, -1).wait_recv()
        copy(ring, h, 2, -1).start()
        copy(ring, h, 1, 1).wait_recv()
        copy(ring, h, 3, 1).start()

    def finish(ring, h):
        copy(ring, h, 2, 2).wait_recv()
        copy(ring, h, 3, 2).wait_recv()

    def open_rings(h):
        send(0, h)
        send(1, h)

    def grow(h):
        forward(0, h)
        send(2, h)
        send(3, h)

    def close_first(h):
        finish(0, h)
        send(4, h)

    def rest(opened, grown):
        opened()
        each(0, 2, lambda h: use(h, place(h, 0, 0)))
        each(0, 2, grow)
        grown()
        each(0, 4, lambda i: use(i // 2, piece(0, i // 2, 2 * (i % 2) - 1)))
        each(0, 2, close_first)
        each(0, 2, lambda h: use(h, piece(0, h, 2)))
        each(1, SIDE + 1, pass_on)
        each(1, SIDE + 1, take_last)
        each(0, 2, drain)

    def pass_on(ring):
        each(0, 2, lambda h: forward(ring, h))
        each(0, 4, lambda i: use(i // 2, piece(ring, i // 2, 2 * (i % 2) - 1)))

    def take_last(ring):
        each(0, 2, lambda h: finish(ring, h))
        each(0, 2, lambda h: use(h, piece(ring, h, 2)))

    def drain(index):
        h = index % 2
        for kind in range(4):
            copy(0, h, kind, 0).wait_send()
        each(1, SIDE + 1, lambda ring: drain_ring(ring, h))

    def drain_ring(ring, h):
        for kind in range(4):
            copy(ring, h, kind, 0).wait_send()

    return open_rings, rest


def kernel(
    dims,
    live_ref,
    lengths_ref,
    gain_hbm,
    taps_hbm,
    rates_hbm,
    residues_hbm,
    skip_hbm,
    x_hbm,
    w_in_hbm,
    w_out_hbm,
    out_ref,
    comb,
    last_blocks,
    x_all,
    w_in,
    sums,
    squares,
    proj,
    query,
    gated,
    ends,
    starts,
    edge,
    mixed,
    g_all,
    out_sum,
    w_stage,
    w_half,
    w_mine,
    gain_ref,
    taps_ref,
    rates_ref,
    weight_ref,
    skip_ref,
    small_sems,
    local_sems,
    shift_sems,
    split_sems,
    deep_sems,
    relay_sems,
    edge_sems,
    x_send,
    x_recv,
    g_send,
    g_recv,
):
    ctx_count, tokens, block, width = dims
    ctx = lax.axis_index("ctx")
    ch = lax.axis_index("ch")
    row = ch // SIDE
    col = lax.rem(ch, SIDE)
    partner = ctx + 1 - 2 * lax.rem(ctx, 2)
    depth_count = ctx_count // 2
    capacity = x_hbm.shape[0] // block
    own_blocks = tokens // block
    features = x_hbm.shape[1]
    part_rows = w_out_hbm.shape[0] // ctx_count
    half = tokens // 2
    modes = rates_ref.shape[0]
    small = [
        pltpu.make_async_copy(source, target, small_sems.at[i])
        for i, (source, target) in enumerate(
            (
                (gain_hbm, gain_ref),
                (taps_hbm, taps_ref),
                (rates_hbm, rates_ref),
                (residues_hbm, weight_ref),
                (skip_hbm, skip_ref),
            )
        )
    ]
    tiles = rates_ref.shape[1] // LANES
    run = tokens // GROUPS

    x_in = pltpu.make_async_copy(x_hbm, comb.at[pl.ds(0, capacity * block)], local_sems.at[0])
    x_in.start()

    def w_part(other, target, sem):
        return pltpu.make_async_copy(
            w_out_hbm.at[
                pl.ds(pl.multiple_of(ctx * part_rows, part_rows), part_rows),
                pl.ds(pl.multiple_of(other * features, features), features),
            ],
            target,
            sem,
        )

    for x in range(SIDE):
        for y in range(SIDE):
            w_part(y * SIDE + x, w_stage.at[x, y], local_sems.at[2 + x * SIDE + y]).start()
    w_load = pltpu.make_async_copy(w_in_hbm, w_in, local_sems.at[1])
    w_load.start()
    for copy in small:
        copy.start()

    barrier = pltpu.get_barrier_semaphore()
    for step in range(1, SIDE):
        pl.semaphore_signal(
            barrier, inc=1, device_id=(ctx, row * SIDE + lax.rem(col + step, SIDE)), device_id_type=MESH
        )
        pl.semaphore_signal(
            barrier, inc=1, device_id=(ctx, lax.rem(row + step, SIDE) * SIDE + col), device_id_type=MESH
        )
    for step in range(1, ctx_count):
        pl.semaphore_signal(
            barrier, inc=1, device_id=(lax.rem(ctx + step, ctx_count), ch), device_id_type=MESH
        )
    sums[...] = jnp.zeros_like(sums)
    squares[...] = jnp.zeros_like(squares)
    out_sum[...] = jnp.zeros_like(out_sum)
    x_in.wait()

    before = jnp.int32(0)
    for owner in range(ctx_count):
        before = before + jnp.where(owner < ctx, live_ref[owner], 0)
    here = live_ref[ctx]
    left_live = live_ref[lax.rem(ctx + ctx_count - 1, ctx_count)]
    first_sent = jnp.maximum(here - 2, 0)
    def pick(which, options):
        value = comb[pl.ds(options[0] * block, block), :]
        for option in options[1:]:
            value = jnp.where(which == option, comb[pl.ds(option * block, block), :], value)
        return value

    for i in range(2):
        last_blocks[pl.ds(i * block, block), :] = pick(first_sent + i, list(range(i, capacity - 1 + i)))
    pl.semaphore_wait(barrier, 2 * (SIDE - 1) + ctx_count - 1)

    after = lax.rem(ctx + 1, ctx_count)
    ahead = lax.rem(ctx + ctx_count - 1, ctx_count)
    to_next = remote(
        last_blocks,
        comb.at[pl.ds(capacity * block, 2 * block)],
        shift_sems.at[0],
        shift_sems.at[1],
        (after, ch),
    )
    to_previous = remote(
        comb.at[pl.ds(0, 2 * block)],
        comb.at[pl.ds((capacity + 2) * block, 2 * block)],
        shift_sems.at[2],
        shift_sems.at[3],
        (ahead, ch),
    )
    to_next.start()
    to_previous.start()

    upper, lower = pl.ds(0, part_rows // 2), pl.ds(part_rows // 2, part_rows // 2)
    for x in range(SIDE):
        for y in range(SIDE):
            w_part(y * SIDE + x, w_stage.at[x, y], local_sems.at[2 + x * SIDE + y]).wait()

    def first_x(step):
        x = lax.rem(col + step, SIDE)
        return remote(
            w_stage.at[x, :, upper],
            w_half.at[0, col],
            split_sems.at[0, 0, step],
            split_sems.at[0, 1, step],
            (ctx, row * SIDE + x),
        )

    def first_y(step):
        y = lax.rem(row + step, SIDE)
        return remote(
            w_stage.at[:, y, lower],
            w_half.at[1, row],
            split_sems.at[1, 0, step],
            split_sems.at[1, 1, step],
            (ctx, y * SIDE + col),
        )

    def then_y(step):
        y = lax.rem(row + step, SIDE)
        return remote(
            w_half.at[0, :, y],
            w_mine.at[ctx, row, :, upper],
            split_sems.at[2, 0, step],
            split_sems.at[2, 1, step],
            (ctx, y * SIDE + col),
        )

    def then_x(step):
        x = lax.rem(col + step, SIDE)
        return remote(
            w_half.at[1, :, x],
            w_mine.at[ctx, :, col, lower],
            split_sems.at[3, 0, step],
            split_sems.at[3, 1, step],
            (ctx, row * SIDE + x),
        )

    def over_depth(step):
        return remote(
            w_mine.at[ctx],
            w_mine.at[ctx],
            deep_sems.at[0, step],
            deep_sems.at[1, step],
            (lax.rem(ctx + 2 * step, ctx_count), ch),
        )

    def to_partner(step):
        held = lax.rem(ctx + 2 * step, ctx_count)
        return remote(
            w_mine.at[held],
            w_mine.at[held],
            relay_sems.at[0, step],
            relay_sems.at[1, step],
            (partner, ch),
        )

    for step in (1, 3, 2):
        first_x(step).start()
        first_y(step).start()
    kept = (
        pltpu.make_async_copy(w_stage.at[col, :, upper], w_half.at[0, col], local_sems.at[0]),
        pltpu.make_async_copy(w_stage.at[:, row, lower], w_half.at[1, row], local_sems.at[2]),
        pltpu.make_async_copy(w_half.at[0, :, row], w_mine.at[ctx, row, :, upper], local_sems.at[3]),
        pltpu.make_async_copy(w_half.at[1, :, col], w_mine.at[ctx, :, col, lower], local_sems.at[4]),
    )
    kept[0].start()
    kept[1].start()

    def fill(h):
        for i in range(h * own_blocks // 2, (h + 1) * own_blocks // 2):
            wanted = ctx * own_blocks + i
            local = list(range(max(i - 2, 0), min(i + 3, capacity)))
            if h == 0:
                other = capacity + left_live - (before - wanted) - jnp.maximum(left_live - 2, 0)
                source = jnp.where(wanted < before, other, wanted - before)
                options = local + [capacity, capacity + 1]
            else:
                other = capacity + 2 + wanted - before - here
                source = jnp.where(wanted >= before + here, other, wanted - before)
                options = local + [capacity + 2, capacity + 3]
            x_all[ch, h, pl.ds((i * block) % half, block), :] = pick(source, options)

    def project(h, g):
        wide = x_all[g, h].astype(jnp.float32)
        squared = wide * wide
        folded = squared[:, :LANES]
        for lane in range(1, features // LANES):
            folded = folded + squared[:, lane * LANES : (lane + 1) * LANES]
        at = pl.ds(pl.multiple_of(h * half, half), half)
        squares[at, :] = squares[at, :] + folded
        deep = pl.ds(pl.multiple_of(g * features, features), features)
        scaled = (wide * gain_ref[:, deep]).astype(jnp.bfloat16)
        for branch in range(BRANCHES):
            sums[branch, at, :] = sums[branch, at, :] + jnp.dot(
                scaled, w_in[branch, deep, :], preferred_element_type=jnp.float32
            )

    def second_leg():
        kept[0].wait()
        kept[1].wait()
        for step in range(1, SIDE):
            first_x(step).wait_recv()
            first_y(step).wait_recv()
        for step in (1, 3, 2):
            then_y(step).start()
            then_x(step).start()
        kept[2].start()
        kept[3].start()
        w_load.wait()
        for copy in small:
            copy.wait()
        doubled = 2.0 * rates_ref[...]
        series = jnp.ones_like(doubled)
        for order in range(8, 1, -1):
            series = 1.0 - doubled * (1.0 / order) * series
        risen = jnp.where(doubled < 0.1, doubled * series, 1.0 - jnp.exp(-doubled))
        weight_ref[...] = weight_ref[...] * jnp.sqrt(risen)

    def third_leg():
        for step in range(1, SIDE):
            then_y(step).wait_recv()
            then_x(step).wait_recv()
        kept[2].wait()
        kept[3].wait()
        for step in range(1, depth_count):
            over_depth(step).start()
        to_partner(0).start()

    open_x, rest_x = plane_gather(x_all, x_send, x_recv, ctx, row, col, project)
    parity = lax.rem(ctx, 2)

    def take(h):
        @pl.when(h == 0)
        def _():
            to_next.wait_recv()
            fill(0)

        @pl.when(h == 1)
        def _():
            to_previous.wait_recv()
            fill(1)

        open_x(h)

    take(1 - parity)
    take(parity)
    rest_x(second_leg, third_leg)
    def scale_rows(begin, count):
        total = jnp.sum(squares[pl.ds(begin, count), :], axis=1, keepdims=True)
        scale = lax.rsqrt(total / width + EPS)
        for branch in range(BRANCHES):
            for tile in range(tiles):
                proj[branch, tile, pl.ds(begin + 8, count), :] = (
                    sums[branch, pl.ds(begin, count), tile * LANES : (tile + 1) * LANES] * scale
                )

    scale_rows(tokens - run, run)
    halo = remote(
        proj.at[:, :, pl.ds(tokens, 8)],
        proj.at[:, :, pl.ds(0, 8)],
        shift_sems.at[4],
        shift_sems.at[5],
        (after, ch),
    )
    halo.start()
    each(0, GROUPS - 1, lambda i: scale_rows(pl.multiple_of(i * run, run), run))
    halo.wait_recv()

    cut_one = lengths_ref[0]
    cut_two = cut_one + lengths_ref[1]
    base = ctx * tokens
    group_start = base + run * lax.broadcasted_iota(jnp.int32, (GROUPS, LANES), 0)

    def keep_at(t):
        token = group_start + t
        begins = (token == 0) | (token == cut_one) | (token == cut_two)
        return jnp.where(begins, 0.0, 1.0).astype(jnp.float32)

    def unbroken(begin, count):
        cut = (begin == 0) | ((cut_one >= begin) & (cut_one < begin + count)) | ((cut_two >= begin) & (cut_two < begin + count))
        return jnp.where(cut, 0.0, 1.0).astype(jnp.float32)

    def spread_row(values):
        return jnp.broadcast_to(values, (GROUPS, LANES))

    run_decay = [jnp.exp(-run * rates_ref[:, pl.ds(tile * LANES, LANES)]) for tile in range(tiles)]
    all_decay = [jnp.exp(-tokens * rates_ref[:, pl.ds(tile * LANES, LANES)]) for tile in range(tiles)]
    unbroken_run = [unbroken(base + run * i, run) for i in range(GROUPS)]

    unbroken_device = [unbroken(jnp.int32(device * tokens), tokens) for device in range(ctx_count)]

    def edge_to(step, tile):
        return remote(
            edge.at[ctx, tile],
            edge.at[ctx, tile],
            edge_sems.at[0, tile, step],
            edge_sems.at[1, tile, step],
            (lax.rem(ctx + step, ctx_count), ch),
        )

    def first_pass(tile):
        lanes = pl.ds(tile * LANES, LANES)
        decays = [spread_row(jnp.exp(-rates_ref[pl.ds(m, 1), lanes])) for m in range(modes)]
        taps = [
            [spread_row(taps_ref[tap, pl.ds(branch, 1), lanes]) for branch in range(BRANCHES)]
            for tap in range(TAPS)
        ]

        def collect(t, carry, decays=decays, taps=taps):
            states, one_back, two_back, keep_before = carry
            keep = keep_at(t)
            far = keep * keep_before
            now = [proj[branch, tile, pl.ds(8 + t, GROUPS, stride=run), :] for branch in range(BRANCHES)]
            parts = [
                taps[0][branch] * now[branch]
                + taps[1][branch] * (keep * one_back[branch])
                + taps[2][branch] * (far * two_back[branch])
                for branch in range(BRANCHES)
            ]
            entered = parts[1] * parts[2]
            query[tile, t] = parts[0]
            gated[tile, t] = entered
            states = [decays[m] * (states[m] * keep) + entered for m in range(modes)]
            return (states, now, one_back, keep)

        first = [proj[branch, tile, pl.ds(7, GROUPS, stride=run), :] for branch in range(BRANCHES)]
        second = [proj[branch, tile, pl.ds(6, GROUPS, stride=run), :] for branch in range(BRANCHES)]
        zero = jnp.zeros((GROUPS, LANES), jnp.float32)
        done = lax.fori_loop(0, run, collect, ([zero] * modes, first, second, keep_at(-1)), unroll=4)
        for m in range(modes):
            ends[tile, pl.ds(m * GROUPS, GROUPS), :] = done[0][m]
        state = jnp.zeros((modes, LANES), jnp.float32)
        for i in range(GROUPS):
            state = ends[tile, pl.ds(i, modes, stride=GROUPS), :] + (unbroken_run[i] * run_decay[tile]) * state
        edge[ctx, tile] = state
        for step in range(1, ctx_count):
            edge_to(step, tile).start()

    def multiply_out(h, g):
        parts = LANES // part_rows
        weights = w_mine[pl.ds(h * parts, parts), g // SIDE, lax.rem(g, SIDE)].reshape(LANES, features)
        out_sum[...] = out_sum[...] + jnp.dot(g_all[g, h], weights, preferred_element_type=jnp.float32)

    open_g, rest_g = plane_gather(g_all, g_send, g_recv, ctx, row, col, multiply_out)

    def second_pass(tile):
        for step in range(1, ctx_count):
            edge_to(step, tile).wait_recv()
        state = jnp.zeros((modes, LANES), jnp.float32)
        for device in range(ctx_count):
            moved = edge[device, tile] + (unbroken_device[device] * all_decay[tile]) * state
            state = jnp.where(device < ctx, moved, state)
        for i in range(GROUPS):
            starts[tile, pl.ds(i, modes, stride=GROUPS), :] = state
            if i < GROUPS - 1:
                state = ends[tile, pl.ds(i, modes, stride=GROUPS), :] + (unbroken_run[i] * run_decay[tile]) * state
        lanes = pl.ds(tile * LANES, LANES)
        decays = [spread_row(jnp.exp(-rates_ref[pl.ds(m, 1), lanes])) for m in range(modes)]
        weights = [spread_row(weight_ref[pl.ds(m, 1), lanes]) for m in range(modes)]
        direct = spread_row(skip_ref[:, lanes])

        def filtered(t, states, decays=decays, weights=weights, direct=direct):
            keep = keep_at(t)
            entered = gated[tile, t]
            states = [decays[m] * (states[m] * keep) + entered for m in range(modes)]
            terms = [weights[m] * states[m] for m in range(modes)] + [direct * entered]
            while len(terms) > 1:
                terms = [
                    terms[k] + terms[k + 1] if k + 1 < len(terms) else terms[k]
                    for k in range(0, len(terms), 2)
                ]
            mixed[tile, pl.ds(t, GROUPS, stride=run), :] = query[tile, t] * terms[0]
            return states

        lax.fori_loop(
            0, run, filtered, [starts[tile, pl.ds(m * GROUPS, GROUPS), :] for m in range(modes)], unroll=4
        )
        g_all[ch, tile] = mixed[tile].astype(jnp.bfloat16)
        open_g(tile)

    for tile in range(tiles):
        first_pass(tile)
    for step in range(1, depth_count):
        over_depth(depth_count - step).wait_recv()
        to_partner(step).start()
    for tile in range(tiles):
        second_pass(tile)

    def last_leg():
        for step in range(1, depth_count):
            to_partner(depth_count - step).wait_recv()
        to_partner(0).wait_recv()

    rest_g(last_leg, lambda: None)
    for h in range(2):
        out_ref[:, pl.ds(h * half, half)] = jnp.transpose(out_sum[pl.ds(h * half, half), :]).astype(jnp.bfloat16)

    to_next.wait_send()
    to_previous.wait_send()
    halo.wait_send()
    for step in range(1, SIDE):
        first_x(step).wait_send()
        first_y(step).wait_send()
        then_y(step).wait_send()
        then_x(step).wait_send()
    for step in range(1, depth_count):
        over_depth(step).wait_send()
    for step in range(depth_count):
        to_partner(step).wait_send()
    for step in range(1, ctx_count):
        for tile in range(tiles):
            edge_to(step, tile).wait_send()


def body(
    x_owned,
    live_blocks,
    seq_lengths,
    norm_gain,
    w_in,
    w_short,
    decay_rates,
    residues,
    skip_gain,
    w_out,
):
    ctx_count = lax.axis_size("ctx")
    ch_count = lax.axis_size("ch")
    width = norm_gain.shape[0]
    features = x_owned.shape[1]
    tokens = x_owned.shape[0] // 2
    block = tokens // 4
    half = tokens // 2
    run = tokens // GROUPS
    modes, channels = decay_rates.shape
    tiles = channels // LANES
    part_rows = channels // ctx_count
    bf16, f32 = jnp.bfloat16, jnp.float32
    smem = pl.BlockSpec(memory_space=pltpu.SMEM)
    vmem = pl.BlockSpec(memory_space=pltpu.VMEM)
    anywhere = pl.BlockSpec(memory_space=pl.ANY)
    dma = pltpu.SemaphoreType.DMA
    flops = 2 * tokens * width * BRANCHES * channels + 2 * tokens * features * ch_count * channels
    return pl.pallas_call(
        functools.partial(kernel, (ctx_count, tokens, block, width)),
        out_shape=jax.ShapeDtypeStruct((features, tokens), bf16),
        in_specs=[smem, smem] + [anywhere] * 8,
        out_specs=vmem,
        scratch_shapes=[
            pltpu.VMEM((x_owned.shape[0] + 4 * block, features), bf16),
            pltpu.VMEM((2 * block, features), bf16),
            pltpu.VMEM((ch_count, 2, half, features), bf16),
            pltpu.VMEM((BRANCHES, width, channels), bf16),
            pltpu.VMEM((BRANCHES, tokens, channels), f32),
            pltpu.VMEM((tokens, LANES), f32),
            pltpu.VMEM((BRANCHES, tiles, tokens + 8, LANES), f32),
            pltpu.VMEM((tiles, run, GROUPS, LANES), f32),
            pltpu.VMEM((tiles, run, GROUPS, LANES), f32),
            pltpu.VMEM((tiles, modes * GROUPS, LANES), f32),
            pltpu.VMEM((tiles, modes * GROUPS, LANES), f32),
            pltpu.VMEM((ctx_count, tiles, modes, LANES), f32),
            pltpu.VMEM((tiles, tokens, LANES), f32),
            pltpu.VMEM((ch_count, tiles, tokens, LANES), bf16),
            pltpu.VMEM((tokens, features), f32),
            pltpu.VMEM((SIDE, SIDE, part_rows, features), bf16),
            pltpu.VMEM((2, SIDE, SIDE, part_rows // 2, features), bf16),
            pltpu.VMEM((ctx_count, SIDE, SIDE, part_rows, features), bf16),
            pltpu.VMEM((1, width), f32),
            pltpu.VMEM((TAPS, BRANCHES, channels), f32),
            pltpu.VMEM((modes, channels), f32),
            pltpu.VMEM((modes, channels), f32),
            pltpu.VMEM((1, channels), f32),
            dma((5,)),
            dma((2 + ch_count,)),
            dma((6,)),
            dma((4, 2, SIDE)),
            dma((2, ctx_count // 2)),
            dma((2, ctx_count // 2)),
            dma((2, tiles, ctx_count)),
            dma((SIDE + 1, 2, 4)),
            dma((SIDE + 1, 2, 4)),
            dma((SIDE + 1, 2, 4)),
            dma((SIDE + 1, 2, 4)),
        ],
        compiler_params=pltpu.CompilerParams(
            collective_id=0, has_side_effects=True, vmem_limit_bytes=56 * 1024 * 1024
        ),
        cost_estimate=pl.CostEstimate(flops=flops, bytes_accessed=18 << 20, transcendentals=0),
    )(
        live_blocks,
        seq_lengths,
        norm_gain.reshape(1, width),
        w_short,
        decay_rates,
        residues,
        skip_gain.reshape(1, channels),
        x_owned,
        w_in,
        w_out,
    )


def solution(mesh):
    return jax.shard_map(
        body,
        mesh=mesh,
        in_specs=(
            P("ctx", "ch"),
            P(),
            P(),
            P(),
            P(None, None, "ch"),
            P(None, None, "ch"),
            P(None, "ch"),
            P(None, "ch"),
            P("ch"),
            P("ch", None),
        ),
        out_specs=P("ch", "ctx"),
        check_vma=False,
    )
```

```python
import functools

import jax
import jax.numpy as jnp
from jax import lax
from jax.experimental import pallas as pl
from jax.experimental.pallas import tpu as pltpu
from jax.sharding import PartitionSpec as P

EPS = 1e-06
TAPS = 3
BRANCHES = 3
SIDE = 4
LANES = 128
GROUPS = 8
MESH = pl.DeviceIdType.MESH


def remote(src, dst, send_sem, recv_sem, device):
    return pltpu.make_async_remote_copy(
        src_ref=src,
        dst_ref=dst,
        send_sem=send_sem,
        recv_sem=recv_sem,
        device_id=device,
        device_id_type=MESH,
    )


def each(lower, upper, step):
    def run(index, carry):
        step(index)
        return carry

    lax.fori_loop(lower, upper, run, 0)


def plane_gather(buf, send_sems, recv_sems, ctx, row, col, use):
    half = buf.shape[2]
    quarter = half // 2
    rows = (pl.ds(0, half), pl.ds(0, half), pl.ds(0, quarter), pl.ds(quarter, quarter))

    def place(h, first, second):
        x = lax.rem(col + (1 - h) * first + h * second + 2 * SIDE, SIDE)
        y = lax.rem(row + (1 - h) * second + h * first + 2 * SIDE, SIDE)
        return y * SIDE + x

    def offset(ring):
        k = ring - 1
        return k + k // 2 - 2 * (k // 3)

    def piece(ring, h, along):
        if isinstance(ring, int) and ring == 0:
            return place(h, along, 0)
        return place(h, offset(ring), along)

    def neighbour(ring, h, along):
        if isinstance(ring, int) and ring == 0:
            return (ctx, place(h, along, 0))
        return (ctx, place(h, 0, along))

    def copy(ring, h, kind, along):
        part = buf.at[piece(ring, h, along), h, rows[kind]]
        return remote(
            part,
            part,
            send_sems.at[ring, h, kind],
            recv_sems.at[ring, h, kind],
            neighbour(ring, h, 1 - 2 * (kind % 2)),
        )

    def send(ring, h):
        copy(ring, h, 0, 0).start()
        copy(ring, h, 1, 0).start()

    def forward(ring, h):
        copy(ring, h, 0, -1).wait_recv()
        copy(ring, h, 2, -1).start()
        copy(ring, h, 1, 1).wait_recv()
        copy(ring, h, 3, 1).start()

    def finish(ring, h):
        copy(ring, h, 2, 2).wait_recv()
        copy(ring, h, 3, 2).wait_recv()

    def open_rings(h):
        send(0, h)
        send(1, h)

    def grow(h):
        forward(0, h)
        send(2, h)
        send(3, h)

    def close_first(h):
        finish(0, h)
        send(4, h)

    def forward_both(ring):
        each(0, 2, lambda h: forward(ring, h))

    def use_sides(ring):
        each(0, 4, lambda i: use(i // 2, piece(ring, i // 2, 2 * (i % 2) - 1)))

    def pass_on(ring):
        forward_both(ring)
        use_sides(ring)

    def take_last(ring):
        each(0, 2, lambda h: finish(ring, h))
        each(0, 2, lambda h: use(h, piece(ring, h, 2)))

    def use_own():
        each(0, 2, lambda h: use(h, place(h, 0, 0)))

    def use_opposite():
        each(0, 2, lambda h: use(h, piece(0, h, 2)))

    def use_as_it_comes(opened, passed):
        opened()
        use_own()
        each(0, 2, grow)
        use_sides(0)
        each(0, 2, close_first)
        use_opposite()
        each(1, SIDE + 1, pass_on)
        passed()
        each(1, SIDE + 1, take_last)
        each(0, 2, drain)

    def use_when_ready(grown, nearly, ready):
        each(0, 2, grow)
        grown()
        each(0, 2, close_first)
        each(1, SIDE, forward_both)
        nearly()
        each(SIDE, SIDE + 1, forward_both)
        ready()
        use_own()
        use_sides(0)
        use_opposite()
        each(1, SIDE + 1, use_sides)
        each(1, SIDE + 1, take_last)
        each(0, 2, drain)

    def drain(index):
        h = index % 2
        for kind in range(4):
            copy(0, h, kind, 0).wait_send()
        each(1, SIDE + 1, lambda ring: drain_ring(ring, h))

    def drain_ring(ring, h):
        for kind in range(4):
            copy(ring, h, kind, 0).wait_send()

    return open_rings, use_as_it_comes, use_when_ready


def kernel(
    dims,
    live_ref,
    lengths_ref,
    gain_hbm,
    taps_hbm,
    rates_hbm,
    residues_hbm,
    skip_hbm,
    x_hbm,
    w_in_hbm,
    w_out_hbm,
    out_ref,
    comb,
    last_blocks,
    x_all,
    w_in,
    sums,
    squares,
    proj,
    query,
    gated,
    ends,
    starts,
    edge,
    mixed,
    g_all,
    out_sum,
    w_stage,
    w_half,
    w_mine,
    gain_ref,
    taps_ref,
    rates_ref,
    weight_ref,
    skip_ref,
    small_sems,
    local_sems,
    shift_sems,
    split_sems,
    deep_sems,
    relay_sems,
    edge_sems,
    x_send,
    x_recv,
    g_send,
    g_recv,
):
    ctx_count, tokens, block, width = dims
    ctx = lax.axis_index("ctx")
    ch = lax.axis_index("ch")
    row = ch // SIDE
    col = lax.rem(ch, SIDE)
    partner = ctx + 1 - 2 * lax.rem(ctx, 2)
    depth_count = ctx_count // 2
    capacity = x_hbm.shape[0] // block
    own_blocks = tokens // block
    features = x_hbm.shape[1]
    part_rows = w_out_hbm.shape[0] // ctx_count
    half = tokens // 2
    modes = rates_ref.shape[0]
    small = [
        pltpu.make_async_copy(source, target, small_sems.at[i])
        for i, (source, target) in enumerate(
            (
                (gain_hbm, gain_ref),
                (taps_hbm, taps_ref),
                (rates_hbm, rates_ref),
                (residues_hbm, weight_ref),
                (skip_hbm, skip_ref),
            )
        )
    ]
    tiles = rates_ref.shape[1] // LANES
    run = tokens // GROUPS

    x_in = pltpu.make_async_copy(x_hbm, comb.at[pl.ds(0, capacity * block)], local_sems.at[0])
    x_in.start()

    def w_part(other, target, sem):
        return pltpu.make_async_copy(
            w_out_hbm.at[
                pl.ds(pl.multiple_of(ctx * part_rows, part_rows), part_rows),
                pl.ds(pl.multiple_of(other * features, features), features),
            ],
            target,
            sem,
        )

    for x in range(SIDE):
        for y in range(SIDE):
            w_part(y * SIDE + x, w_stage.at[x, y], local_sems.at[2 + x * SIDE + y]).start()
    w_load = pltpu.make_async_copy(w_in_hbm, w_in, local_sems.at[1])
    w_load.start()
    for copy in small:
        copy.start()

    barrier = pltpu.get_barrier_semaphore()
    for step in range(1, SIDE):
        pl.semaphore_signal(
            barrier, inc=1, device_id=(ctx, row * SIDE + lax.rem(col + step, SIDE)), device_id_type=MESH
        )
        pl.semaphore_signal(
            barrier, inc=1, device_id=(ctx, lax.rem(row + step, SIDE) * SIDE + col), device_id_type=MESH
        )
    for step in range(1, ctx_count):
        pl.semaphore_signal(
            barrier, inc=1, device_id=(lax.rem(ctx + step, ctx_count), ch), device_id_type=MESH
        )
    sums[...] = jnp.zeros_like(sums)
    squares[...] = jnp.zeros_like(squares)
    out_sum[...] = jnp.zeros_like(out_sum)
    x_in.wait()

    before = jnp.int32(0)
    for owner in range(ctx_count):
        before = before + jnp.where(owner < ctx, live_ref[owner], 0)
    here = live_ref[ctx]
    left_live = live_ref[lax.rem(ctx + ctx_count - 1, ctx_count)]
    first_sent = jnp.maximum(here - 2, 0)
    def pick(which, options):
        value = comb[pl.ds(options[0] * block, block), :]
        for option in options[1:]:
            value = jnp.where(which == option, comb[pl.ds(option * block, block), :], value)
        return value

    for i in range(2):
        last_blocks[pl.ds(i * block, block), :] = pick(first_sent + i, list(range(i, capacity - 1 + i)))
    pl.semaphore_wait(barrier, 2 * (SIDE - 1) + ctx_count - 1)

    after = lax.rem(ctx + 1, ctx_count)
    ahead = lax.rem(ctx + ctx_count - 1, ctx_count)
    to_next = remote(
        last_blocks,
        comb.at[pl.ds(capacity * block, 2 * block)],
        shift_sems.at[0],
        shift_sems.at[1],
        (after, ch),
    )
    to_previous = remote(
        comb.at[pl.ds(0, 2 * block)],
        comb.at[pl.ds((capacity + 2) * block, 2 * block)],
        shift_sems.at[2],
        shift_sems.at[3],
        (ahead, ch),
    )
    to_next.start()
    to_previous.start()

    upper, lower = pl.ds(0, part_rows // 2), pl.ds(part_rows // 2, part_rows // 2)
    for x in range(SIDE):
        for y in range(SIDE):
            w_part(y * SIDE + x, w_stage.at[x, y], local_sems.at[2 + x * SIDE + y]).wait()

    def first_x(step):
        x = lax.rem(col + step, SIDE)
        return remote(
            w_stage.at[x, :, upper],
            w_half.at[0, col],
            split_sems.at[0, 0, step],
            split_sems.at[0, 1, step],
            (ctx, row * SIDE + x),
        )

    def first_y(step):
        y = lax.rem(row + step, SIDE)
        return remote(
            w_stage.at[:, y, lower],
            w_half.at[1, row],
            split_sems.at[1, 0, step],
            split_sems.at[1, 1, step],
            (ctx, y * SIDE + col),
        )

    def then_y(step):
        y = lax.rem(row + step, SIDE)
        return remote(
            w_half.at[0, :, y],
            w_mine.at[ctx, row, :, upper],
            split_sems.at[2, 0, step],
            split_sems.at[2, 1, step],
            (ctx, y * SIDE + col),
        )

    def then_x(step):
        x = lax.rem(col + step, SIDE)
        return remote(
            w_half.at[1, :, x],
            w_mine.at[ctx, :, col, lower],
            split_sems.at[3, 0, step],
            split_sems.at[3, 1, step],
            (ctx, row * SIDE + x),
        )

    def over_depth(kind):
        shift = 2 * (1 - 2 * (kind % 2))
        target = lax.rem(ctx + ctx_count + shift, ctx_count)
        held = ctx if kind < 2 else lax.rem(ctx + ctx_count - shift, ctx_count)
        part = w_mine.at[held, pl.ds((0, 0, 0, SIDE // 2)[kind], (SIDE, SIDE, SIDE // 2, SIDE // 2)[kind])]
        return remote(part, part, deep_sems.at[0, kind], deep_sems.at[1, kind], (target, ch))

    def to_partner(step):
        held = lax.rem(ctx + 2 * step, ctx_count)
        return remote(
            w_mine.at[held],
            w_mine.at[held],
            relay_sems.at[0, step],
            relay_sems.at[1, step],
            (partner, ch),
        )

    kept = (
        pltpu.make_async_copy(w_stage.at[col, :, upper], w_half.at[0, col], local_sems.at[0]),
        pltpu.make_async_copy(w_stage.at[:, row, lower], w_half.at[1, row], local_sems.at[2]),
        pltpu.make_async_copy(w_half.at[0, :, row], w_mine.at[ctx, row, :, upper], local_sems.at[3]),
        pltpu.make_async_copy(w_half.at[1, :, col], w_mine.at[ctx, :, col, lower], local_sems.at[4]),
    )
    def fill(h):
        for i in range(h * own_blocks // 2, (h + 1) * own_blocks // 2):
            wanted = ctx * own_blocks + i
            local = list(range(max(i - 2, 0), min(i + 3, capacity)))
            if h == 0:
                other = capacity + left_live - (before - wanted) - jnp.maximum(left_live - 2, 0)
                source = jnp.where(wanted < before, other, wanted - before)
                options = local + [capacity, capacity + 1]
            else:
                other = capacity + 2 + wanted - before - here
                source = jnp.where(wanted >= before + here, other, wanted - before)
                options = local + [capacity + 2, capacity + 3]
            x_all[ch, h, pl.ds((i * block) % half, block), :] = pick(source, options)

    def project(h, g):
        wide = x_all[g, h].astype(jnp.float32)
        squared = wide * wide
        folded = squared[:, :LANES]
        for lane in range(1, features // LANES):
            folded = folded + squared[:, lane * LANES : (lane + 1) * LANES]
        at = pl.ds(pl.multiple_of(h * half, half), half)
        squares[at, :] = squares[at, :] + folded
        deep = pl.ds(pl.multiple_of(g * features, features), features)
        scaled = (wide * gain_ref[:, deep]).astype(jnp.bfloat16)
        for branch in range(BRANCHES):
            sums[branch, at, :] = sums[branch, at, :] + jnp.dot(
                scaled, w_in[branch, deep, :], preferred_element_type=jnp.float32
            )

    def ready_weights():
        w_load.wait()
        for copy in small:
            copy.wait()
        doubled = 2.0 * rates_ref[...]
        series = jnp.ones_like(doubled)
        for order in range(8, 1, -1):
            series = 1.0 - doubled * (1.0 / order) * series
        risen = jnp.where(doubled < 0.1, doubled * series, 1.0 - jnp.exp(-doubled))
        weight_ref[...] = weight_ref[...] * jnp.sqrt(risen)

    def first_leg():
        for step in (1, 3, 2):
            first_x(step).start()
            first_y(step).start()
        kept[0].start()
        kept[1].start()

    def second_leg():
        kept[0].wait()
        kept[1].wait()
        for step in range(1, SIDE):
            first_x(step).wait_recv()
            first_y(step).wait_recv()
        for step in (1, 3, 2):
            then_y(step).start()
            then_x(step).start()
        kept[2].start()
        kept[3].start()

    def third_leg():
        for step in range(1, SIDE):
            then_y(step).wait_recv()
            then_x(step).wait_recv()
        kept[2].wait()
        kept[3].wait()
        over_depth(0).start()
        over_depth(1).start()
        to_partner(0).start()

    def fourth_leg():
        over_depth(0).wait_recv()
        over_depth(2).start()
        over_depth(1).wait_recv()
        over_depth(3).start()
        to_partner(1).start()
        to_partner(depth_count - 1).start()

    def fifth_leg():
        over_depth(2).wait_recv()
        over_depth(3).wait_recv()
        to_partner(2).start()

    open_x, rest_x, _ = plane_gather(x_all, x_send, x_recv, ctx, row, col, project)
    parity = lax.rem(ctx, 2)

    def take(h):
        @pl.when(h == 0)
        def _():
            to_next.wait_recv()
            fill(0)

        @pl.when(h == 1)
        def _():
            to_previous.wait_recv()
            fill(1)

        open_x(h)

    take(1 - parity)
    take(parity)
    rest_x(ready_weights, first_leg)
    def scale_rows(begin, count):
        total = jnp.sum(squares[pl.ds(begin, count), :], axis=1, keepdims=True)
        scale = lax.rsqrt(total / width + EPS)
        for branch in range(BRANCHES):
            for tile in range(tiles):
                proj[branch, tile, pl.ds(begin + 8, count), :] = (
                    sums[branch, pl.ds(begin, count), tile * LANES : (tile + 1) * LANES] * scale
                )

    scale_rows(tokens - run, run)
    halo = remote(
        proj.at[:, :, pl.ds(tokens, 8)],
        proj.at[:, :, pl.ds(0, 8)],
        shift_sems.at[4],
        shift_sems.at[5],
        (after, ch),
    )
    halo.start()
    each(0, GROUPS - 1, lambda i: scale_rows(pl.multiple_of(i * run, run), run))
    second_leg()
    halo.wait_recv()

    cut_one = lengths_ref[0]
    cut_two = cut_one + lengths_ref[1]
    base = ctx * tokens
    group_start = base + run * lax.broadcasted_iota(jnp.int32, (GROUPS, LANES), 0)

    def keep_at(t):
        token = group_start + t
        begins = (token == 0) | (token == cut_one) | (token == cut_two)
        return jnp.where(begins, 0.0, 1.0).astype(jnp.float32)

    def unbroken(begin, count):
        cut = (begin == 0) | ((cut_one >= begin) & (cut_one < begin + count)) | ((cut_two >= begin) & (cut_two < begin + count))
        return jnp.where(cut, 0.0, 1.0).astype(jnp.float32)

    def spread_row(values):
        return jnp.broadcast_to(values, (GROUPS, LANES))

    run_decay = [jnp.exp(-run * rates_ref[:, pl.ds(tile * LANES, LANES)]) for tile in range(tiles)]
    all_decay = [jnp.exp(-tokens * rates_ref[:, pl.ds(tile * LANES, LANES)]) for tile in range(tiles)]
    unbroken_run = [unbroken(base + run * i, run) for i in range(GROUPS)]

    unbroken_device = [unbroken(jnp.int32(device * tokens), tokens) for device in range(ctx_count)]

    def edge_to(step, tile):
        return remote(
            edge.at[ctx, tile],
            edge.at[ctx, tile],
            edge_sems.at[0, tile, step],
            edge_sems.at[1, tile, step],
            (lax.rem(ctx + step, ctx_count), ch),
        )

    def first_pass(tile):
        lanes = pl.ds(tile * LANES, LANES)
        decays = [spread_row(jnp.exp(-rates_ref[pl.ds(m, 1), lanes])) for m in range(modes)]
        taps = [
            [spread_row(taps_ref[tap, pl.ds(branch, 1), lanes]) for branch in range(BRANCHES)]
            for tap in range(TAPS)
        ]

        def collect(t, carry, decays=decays, taps=taps):
            states, one_back, two_back, keep_before = carry
            keep = keep_at(t)
            far = keep * keep_before
            now = [proj[branch, tile, pl.ds(8 + t, GROUPS, stride=run), :] for branch in range(BRANCHES)]
            parts = [
                taps[0][branch] * now[branch]
                + taps[1][branch] * (keep * one_back[branch])
                + taps[2][branch] * (far * two_back[branch])
                for branch in range(BRANCHES)
            ]
            entered = parts[1] * parts[2]
            query[tile, t] = parts[0]
            gated[tile, t] = entered
            states = [decays[m] * (states[m] * keep) + entered for m in range(modes)]
            return (states, now, one_back, keep)

        first = [proj[branch, tile, pl.ds(7, GROUPS, stride=run), :] for branch in range(BRANCHES)]
        second = [proj[branch, tile, pl.ds(6, GROUPS, stride=run), :] for branch in range(BRANCHES)]
        zero = jnp.zeros((GROUPS, LANES), jnp.float32)
        done = lax.fori_loop(0, run, collect, ([zero] * modes, first, second, keep_at(-1)), unroll=4)
        for m in range(modes):
            ends[tile, pl.ds(m * GROUPS, GROUPS), :] = done[0][m]
        state = jnp.zeros((modes, LANES), jnp.float32)
        for i in range(GROUPS):
            state = ends[tile, pl.ds(i, modes, stride=GROUPS), :] + (unbroken_run[i] * run_decay[tile]) * state
        edge[ctx, tile] = state
        for step in range(1, ctx_count):
            edge_to(step, tile).start()

    def multiply_out(h, g):
        parts = LANES // part_rows
        weights = w_mine[pl.ds(h * parts, parts), g // SIDE, lax.rem(g, SIDE)].reshape(LANES, features)
        out_sum[...] = out_sum[...] + jnp.dot(g_all[g, h], weights, preferred_element_type=jnp.float32)

    open_g, _, rest_g = plane_gather(g_all, g_send, g_recv, ctx, row, col, multiply_out)

    def second_pass(tile):
        for step in range(1, ctx_count):
            edge_to(step, tile).wait_recv()
        state = jnp.zeros((modes, LANES), jnp.float32)
        for device in range(ctx_count):
            moved = edge[device, tile] + (unbroken_device[device] * all_decay[tile]) * state
            state = jnp.where(device < ctx, moved, state)
        for i in range(GROUPS):
            starts[tile, pl.ds(i, modes, stride=GROUPS), :] = state
            if i < GROUPS - 1:
                state = ends[tile, pl.ds(i, modes, stride=GROUPS), :] + (unbroken_run[i] * run_decay[tile]) * state
        lanes = pl.ds(tile * LANES, LANES)
        decays = [spread_row(jnp.exp(-rates_ref[pl.ds(m, 1), lanes])) for m in range(modes)]
        weights = [spread_row(weight_ref[pl.ds(m, 1), lanes]) for m in range(modes)]
        direct = spread_row(skip_ref[:, lanes])

        def filtered(t, states, decays=decays, weights=weights, direct=direct):
            keep = keep_at(t)
            entered = gated[tile, t]
            states = [decays[m] * (states[m] * keep) + entered for m in range(modes)]
            terms = [weights[m] * states[m] for m in range(modes)] + [direct * entered]
            while len(terms) > 1:
                terms = [
                    terms[k] + terms[k + 1] if k + 1 < len(terms) else terms[k]
                    for k in range(0, len(terms), 2)
                ]
            mixed[tile, pl.ds(t, GROUPS, stride=run), :] = query[tile, t] * terms[0]
            return states

        lax.fori_loop(
            0, run, filtered, [starts[tile, pl.ds(m * GROUPS, GROUPS), :] for m in range(modes)], unroll=4
        )
        g_all[ch, tile] = mixed[tile].astype(jnp.bfloat16)
        open_g(tile)

    for tile in range(tiles):
        first_pass(tile)
    third_leg()
    for tile in range(tiles):
        second_pass(tile)

    def last_leg():
        for step in range(1, depth_count):
            to_partner(depth_count - step).wait_recv()
        to_partner(0).wait_recv()

    rest_g(fourth_leg, fifth_leg, last_leg)
    for h in range(2):
        out_ref[:, pl.ds(h * half, half)] = jnp.transpose(out_sum[pl.ds(h * half, half), :]).astype(jnp.bfloat16)

    to_next.wait_send()
    to_previous.wait_send()
    halo.wait_send()
    for step in range(1, SIDE):
        first_x(step).wait_send()
        first_y(step).wait_send()
        then_y(step).wait_send()
        then_x(step).wait_send()
    for kind in range(4):
        over_depth(kind).wait_send()
    for step in range(depth_count):
        to_partner(step).wait_send()
    for step in range(1, ctx_count):
        for tile in range(tiles):
            edge_to(step, tile).wait_send()


def body(
    x_owned,
    live_blocks,
    seq_lengths,
    norm_gain,
    w_in,
    w_short,
    decay_rates,
    residues,
    skip_gain,
    w_out,
):
    ctx_count = lax.axis_size("ctx")
    ch_count = lax.axis_size("ch")
    width = norm_gain.shape[0]
    features = x_owned.shape[1]
    tokens = x_owned.shape[0] // 2
    block = tokens // 4
    half = tokens // 2
    run = tokens // GROUPS
    modes, channels = decay_rates.shape
    tiles = channels // LANES
    part_rows = channels // ctx_count
    bf16, f32 = jnp.bfloat16, jnp.float32
    smem = pl.BlockSpec(memory_space=pltpu.SMEM)
    vmem = pl.BlockSpec(memory_space=pltpu.VMEM)
    anywhere = pl.BlockSpec(memory_space=pl.ANY)
    dma = pltpu.SemaphoreType.DMA
    flops = 2 * tokens * width * BRANCHES * channels + 2 * tokens * features * ch_count * channels
    return pl.pallas_call(
        functools.partial(kernel, (ctx_count, tokens, block, width)),
        out_shape=jax.ShapeDtypeStruct((features, tokens), bf16),
        in_specs=[smem, smem] + [anywhere] * 8,
        out_specs=vmem,
        scratch_shapes=[
            pltpu.VMEM((x_owned.shape[0] + 4 * block, features), bf16),
            pltpu.VMEM((2 * block, features), bf16),
            pltpu.VMEM((ch_count, 2, half, features), bf16),
            pltpu.VMEM((BRANCHES, width, channels), bf16),
            pltpu.VMEM((BRANCHES, tokens, channels), f32),
            pltpu.VMEM((tokens, LANES), f32),
            pltpu.VMEM((BRANCHES, tiles, tokens + 8, LANES), f32),
            pltpu.VMEM((tiles, run, GROUPS, LANES), f32),
            pltpu.VMEM((tiles, run, GROUPS, LANES), f32),
            pltpu.VMEM((tiles, modes * GROUPS, LANES), f32),
            pltpu.VMEM((tiles, modes * GROUPS, LANES), f32),
            pltpu.VMEM((ctx_count, tiles, modes, LANES), f32),
            pltpu.VMEM((tiles, tokens, LANES), f32),
            pltpu.VMEM((ch_count, tiles, tokens, LANES), bf16),
            pltpu.VMEM((tokens, features), f32),
            pltpu.VMEM((SIDE, SIDE, part_rows, features), bf16),
            pltpu.VMEM((2, SIDE, SIDE, part_rows // 2, features), bf16),
            pltpu.VMEM((ctx_count, SIDE, SIDE, part_rows, features), bf16),
            pltpu.VMEM((1, width), f32),
            pltpu.VMEM((TAPS, BRANCHES, channels), f32),
            pltpu.VMEM((modes, channels), f32),
            pltpu.VMEM((modes, channels), f32),
            pltpu.VMEM((1, channels), f32),
            dma((5,)),
            dma((2 + ch_count,)),
            dma((6,)),
            dma((4, 2, SIDE)),
            dma((2, 4)),
            dma((2, ctx_count // 2)),
            dma((2, tiles, ctx_count)),
            dma((SIDE + 1, 2, 4)),
            dma((SIDE + 1, 2, 4)),
            dma((SIDE + 1, 2, 4)),
            dma((SIDE + 1, 2, 4)),
        ],
        compiler_params=pltpu.CompilerParams(
            collective_id=0, has_side_effects=True, vmem_limit_bytes=56 * 1024 * 1024
        ),
        cost_estimate=pl.CostEstimate(flops=flops, bytes_accessed=18 << 20, transcendentals=0),
    )(
        live_blocks,
        seq_lengths,
        norm_gain.reshape(1, width),
        w_short,
        decay_rates,
        residues,
        skip_gain.reshape(1, channels),
        x_owned,
        w_in,
        w_out,
    )


def solution(mesh):
    return jax.shard_map(
        body,
        mesh=mesh,
        in_specs=(
            P("ctx", "ch"),
            P(),
            P(),
            P(),
            P(None, None, "ch"),
            P(None, None, "ch"),
            P(None, "ch"),
            P(None, "ch"),
            P("ch"),
            P("ch", None),
        ),
        out_specs=P("ch", "ctx"),
        check_vma=False,
    )
```

```python
import functools

import jax
import jax.numpy as jnp
from jax import lax
from jax.experimental import pallas as pl
from jax.experimental.pallas import tpu as pltpu
from jax.sharding import PartitionSpec as P

EPS = 1e-06
TAPS = 3
BRANCHES = 3
SIDE = 4
LANES = 128
GROUPS = 8
MESH = pl.DeviceIdType.MESH


def remote(src, dst, send_sem, recv_sem, device):
    return pltpu.make_async_remote_copy(
        src_ref=src,
        dst_ref=dst,
        send_sem=send_sem,
        recv_sem=recv_sem,
        device_id=device,
        device_id_type=MESH,
    )


def each(lower, upper, step):
    def run(index, carry):
        step(index)
        return carry

    lax.fori_loop(lower, upper, run, 0)


def plane_gather(buf, send_sems, recv_sems, ctx, row, col, use):
    half = buf.shape[2]
    quarter = half // 2
    rows = (pl.ds(0, half), pl.ds(0, half), pl.ds(0, quarter), pl.ds(quarter, quarter))

    def place(h, first, second):
        x = lax.rem(col + (1 - h) * first + h * second + 2 * SIDE, SIDE)
        y = lax.rem(row + (1 - h) * second + h * first + 2 * SIDE, SIDE)
        return y * SIDE + x

    def offset(ring):
        k = ring - 1
        return k + k // 2 - 2 * (k // 3)

    def piece(ring, h, along):
        if isinstance(ring, int) and ring == 0:
            return place(h, along, 0)
        return place(h, offset(ring), along)

    def neighbour(ring, h, along):
        if isinstance(ring, int) and ring == 0:
            return (ctx, place(h, along, 0))
        return (ctx, place(h, 0, along))

    def copy(ring, h, kind, along):
        part = buf.at[piece(ring, h, along), h, rows[kind]]
        return remote(
            part,
            part,
            send_sems.at[ring, h, kind],
            recv_sems.at[ring, h, kind],
            neighbour(ring, h, 1 - 2 * (kind % 2)),
        )

    def send(ring, h):
        copy(ring, h, 0, 0).start()
        copy(ring, h, 1, 0).start()

    def forward(ring, h):
        copy(ring, h, 0, -1).wait_recv()
        copy(ring, h, 2, -1).start()
        copy(ring, h, 1, 1).wait_recv()
        copy(ring, h, 3, 1).start()

    def finish(ring, h):
        copy(ring, h, 2, 2).wait_recv()
        copy(ring, h, 3, 2).wait_recv()

    def open_rings(h):
        send(0, h)
        send(1, h)

    def grow(h):
        forward(0, h)
        send(2, h)
        send(3, h)

    def close_first(h):
        finish(0, h)
        send(4, h)

    def rest(opened, grown):
        opened()
        each(0, 2, lambda h: use(h, place(h, 0, 0)))
        each(0, 2, grow)
        grown()
        each(0, 4, lambda i: use(i // 2, piece(0, i // 2, 2 * (i % 2) - 1)))
        each(0, 2, close_first)
        each(0, 2, lambda h: use(h, piece(0, h, 2)))
        each(1, SIDE + 1, pass_on)
        each(1, SIDE + 1, take_last)
        each(0, 2, drain)

    def pass_on(ring):
        each(0, 2, lambda h: forward(ring, h))
        each(0, 4, lambda i: use(i // 2, piece(ring, i // 2, 2 * (i % 2) - 1)))

    def take_last(ring):
        each(0, 2, lambda h: finish(ring, h))
        each(0, 2, lambda h: use(h, piece(ring, h, 2)))

    def drain(index):
        h = index % 2
        for kind in range(4):
            copy(0, h, kind, 0).wait_send()
        each(1, SIDE + 1, lambda ring: drain_ring(ring, h))

    def drain_ring(ring, h):
        for kind in range(4):
            copy(ring, h, kind, 0).wait_send()

    return open_rings, rest


def kernel(
    dims,
    live_ref,
    lengths_ref,
    gain_hbm,
    taps_hbm,
    rates_hbm,
    residues_hbm,
    skip_hbm,
    x_hbm,
    w_in_hbm,
    w_out_hbm,
    out_ref,
    comb,
    last_blocks,
    x_all,
    w_in,
    sums,
    squares,
    proj,
    query,
    gated,
    ends,
    starts,
    edge,
    mixed,
    g_all,
    out_sum,
    w_stage,
    w_half,
    w_mine,
    gain_ref,
    taps_ref,
    rates_ref,
    weight_ref,
    skip_ref,
    small_sems,
    local_sems,
    shift_sems,
    split_sems,
    deep_sems,
    relay_sems,
    edge_sems,
    x_send,
    x_recv,
    g_send,
    g_recv,
):
    ctx_count, tokens, block, width = dims
    ctx = lax.axis_index("ctx")
    ch = lax.axis_index("ch")
    row = ch // SIDE
    col = lax.rem(ch, SIDE)
    partner = ctx + 1 - 2 * lax.rem(ctx, 2)
    depth_count = ctx_count // 2
    capacity = x_hbm.shape[0] // block
    own_blocks = tokens // block
    features = x_hbm.shape[1]
    part_rows = w_out_hbm.shape[0] // ctx_count
    half = tokens // 2
    modes = rates_ref.shape[0]
    small = [
        pltpu.make_async_copy(source, target, small_sems.at[i])
        for i, (source, target) in enumerate(
            (
                (gain_hbm, gain_ref),
                (taps_hbm, taps_ref),
                (rates_hbm, rates_ref),
                (residues_hbm, weight_ref),
                (skip_hbm, skip_ref),
            )
        )
    ]
    tiles = rates_ref.shape[1] // LANES
    run = tokens // GROUPS

    x_in = pltpu.make_async_copy(x_hbm, comb.at[pl.ds(0, capacity * block)], local_sems.at[0])
    x_in.start()

    def w_part(other, target, sem):
        return pltpu.make_async_copy(
            w_out_hbm.at[
                pl.ds(pl.multiple_of(ctx * part_rows, part_rows), part_rows),
                pl.ds(pl.multiple_of(other * features, features), features),
            ],
            target,
            sem,
        )

    for x in range(SIDE):
        for y in range(SIDE):
            w_part(y * SIDE + x, w_stage.at[x, y], local_sems.at[2 + x * SIDE + y]).start()
    w_load = pltpu.make_async_copy(w_in_hbm, w_in, local_sems.at[1])
    w_load.start()
    for copy in small:
        copy.start()

    barrier = pltpu.get_barrier_semaphore()
    for step in range(1, SIDE):
        pl.semaphore_signal(
            barrier, inc=1, device_id=(ctx, row * SIDE + lax.rem(col + step, SIDE)), device_id_type=MESH
        )
        pl.semaphore_signal(
            barrier, inc=1, device_id=(ctx, lax.rem(row + step, SIDE) * SIDE + col), device_id_type=MESH
        )
    for step in range(1, ctx_count):
        pl.semaphore_signal(
            barrier, inc=1, device_id=(lax.rem(ctx + step, ctx_count), ch), device_id_type=MESH
        )
    sums[...] = jnp.zeros_like(sums)
    squares[...] = jnp.zeros_like(squares)
    out_sum[...] = jnp.zeros_like(out_sum)
    x_in.wait()

    before = jnp.int32(0)
    for owner in range(ctx_count):
        before = before + jnp.where(owner < ctx, live_ref[owner], 0)
    here = live_ref[ctx]
    left_live = live_ref[lax.rem(ctx + ctx_count - 1, ctx_count)]
    first_sent = jnp.maximum(here - 2, 0)
    def pick(which, options):
        value = comb[pl.ds(options[0] * block, block), :]
        for option in options[1:]:
            value = jnp.where(which == option, comb[pl.ds(option * block, block), :], value)
        return value

    for i in range(2):
        last_blocks[pl.ds(i * block, block), :] = pick(first_sent + i, list(range(i, capacity - 1 + i)))
    pl.semaphore_wait(barrier, 2 * (SIDE - 1) + ctx_count - 1)

    after = lax.rem(ctx + 1, ctx_count)
    ahead = lax.rem(ctx + ctx_count - 1, ctx_count)
    to_next = remote(
        last_blocks,
        comb.at[pl.ds(capacity * block, 2 * block)],
        shift_sems.at[0],
        shift_sems.at[1],
        (after, ch),
    )
    to_previous = remote(
        comb.at[pl.ds(0, 2 * block)],
        comb.at[pl.ds((capacity + 2) * block, 2 * block)],
        shift_sems.at[2],
        shift_sems.at[3],
        (ahead, ch),
    )
    to_next.start()
    to_previous.start()

    upper, lower = pl.ds(0, part_rows // 2), pl.ds(part_rows // 2, part_rows // 2)
    for x in range(SIDE):
        for y in range(SIDE):
            w_part(y * SIDE + x, w_stage.at[x, y], local_sems.at[2 + x * SIDE + y]).wait()

    def first_x(step):
        x = lax.rem(col + step, SIDE)
        return remote(
            w_stage.at[x, :, upper],
            w_half.at[0, col],
            split_sems.at[0, 0, step],
            split_sems.at[0, 1, step],
            (ctx, row * SIDE + x),
        )

    def first_y(step):
        y = lax.rem(row + step, SIDE)
        return remote(
            w_stage.at[:, y, lower],
            w_half.at[1, row],
            split_sems.at[1, 0, step],
            split_sems.at[1, 1, step],
            (ctx, y * SIDE + col),
        )

    def then_y(step):
        y = lax.rem(row + step, SIDE)
        return remote(
            w_half.at[0, :, y],
            w_mine.at[ctx, row, :, upper],
            split_sems.at[2, 0, step],
            split_sems.at[2, 1, step],
            (ctx, y * SIDE + col),
        )

    def then_x(step):
        x = lax.rem(col + step, SIDE)
        return remote(
            w_half.at[1, :, x],
            w_mine.at[ctx, :, col, lower],
            split_sems.at[3, 0, step],
            split_sems.at[3, 1, step],
            (ctx, row * SIDE + x),
        )

    def over_depth(step):
        return remote(
            w_mine.at[ctx],
            w_mine.at[ctx],
            deep_sems.at[0, step],
            deep_sems.at[1, step],
            (lax.rem(ctx + 2 * step, ctx_count), ch),
        )

    def to_partner(step):
        held = lax.rem(ctx + 2 * step, ctx_count)
        return remote(
            w_mine.at[held],
            w_mine.at[held],
            relay_sems.at[0, step],
            relay_sems.at[1, step],
            (partner, ch),
        )

    for step in (1, 3, 2):
        first_x(step).start()
        first_y(step).start()
    kept = (
        pltpu.make_async_copy(w_stage.at[col, :, upper], w_half.at[0, col], local_sems.at[0]),
        pltpu.make_async_copy(w_stage.at[:, row, lower], w_half.at[1, row], local_sems.at[2]),
        pltpu.make_async_copy(w_half.at[0, :, row], w_mine.at[ctx, row, :, upper], local_sems.at[3]),
        pltpu.make_async_copy(w_half.at[1, :, col], w_mine.at[ctx, :, col, lower], local_sems.at[4]),
    )
    kept[0].start()
    kept[1].start()

    def fill(h):
        for i in range(h * own_blocks // 2, (h + 1) * own_blocks // 2):
            wanted = ctx * own_blocks + i
            local = list(range(max(i - 2, 0), min(i + 3, capacity)))
            if h == 0:
                other = capacity + left_live - (before - wanted) - jnp.maximum(left_live - 2, 0)
                source = jnp.where(wanted < before, other, wanted - before)
                options = local + [capacity, capacity + 1]
            else:
                other = capacity + 2 + wanted - before - here
                source = jnp.where(wanted >= before + here, other, wanted - before)
                options = local + [capacity + 2, capacity + 3]
            x_all[ch, h, pl.ds((i * block) % half, block), :] = pick(source, options)

    def project(h, g):
        wide = x_all[g, h].astype(jnp.float32)
        squared = wide * wide
        folded = squared[:, :LANES]
        for lane in range(1, features // LANES):
            folded = folded + squared[:, lane * LANES : (lane + 1) * LANES]
        at = pl.ds(pl.multiple_of(h * half, half), half)
        squares[at, :] = squares[at, :] + folded
        deep = pl.ds(pl.multiple_of(g * features, features), features)
        scaled = (wide * gain_ref[:, deep]).astype(jnp.bfloat16)
        for branch in range(BRANCHES):
            sums[branch, at, :] = sums[branch, at, :] + jnp.dot(
                scaled, w_in[branch, deep, :], preferred_element_type=jnp.float32
            )

    def second_leg():
        kept[0].wait()
        kept[1].wait()
        for step in range(1, SIDE):
            first_x(step).wait_recv()
            first_y(step).wait_recv()
        for step in (1, 3, 2):
            then_y(step).start()
            then_x(step).start()
        kept[2].start()
        kept[3].start()
        w_load.wait()
        for copy in small:
            copy.wait()
        doubled = 2.0 * rates_ref[...]
        series = jnp.ones_like(doubled)
        for order in range(8, 1, -1):
            series = 1.0 - doubled * (1.0 / order) * series
        risen = jnp.where(doubled < 0.1, doubled * series, 1.0 - jnp.exp(-doubled))
        weight_ref[...] = weight_ref[...] * jnp.sqrt(risen)

    def third_leg():
        for step in range(1, SIDE):
            then_y(step).wait_recv()
            then_x(step).wait_recv()
        kept[2].wait()
        kept[3].wait()
        for step in range(1, depth_count):
            over_depth(step).start()
        to_partner(0).start()

    open_x, rest_x = plane_gather(x_all, x_send, x_recv, ctx, row, col, project)
    parity = lax.rem(ctx, 2)

    def take(h):
        @pl.when(h == 0)
        def _():
            to_next.wait_recv()
            fill(0)

        @pl.when(h == 1)
        def _():
            to_previous.wait_recv()
            fill(1)

        open_x(h)

    take(1 - parity)
    take(parity)
    rest_x(second_leg, third_leg)
    def scale_rows(begin, count):
        total = jnp.sum(squares[pl.ds(begin, count), :], axis=1, keepdims=True)
        scale = lax.rsqrt(total / width + EPS)
        for branch in range(BRANCHES):
            for tile in range(tiles):
                proj[branch, tile, pl.ds(begin + 8, count), :] = (
                    sums[branch, pl.ds(begin, count), tile * LANES : (tile + 1) * LANES] * scale
                )

    scale_rows(tokens - run, run)
    halo = remote(
        proj.at[:, :, pl.ds(tokens, 8)],
        proj.at[:, :, pl.ds(0, 8)],
        shift_sems.at[4],
        shift_sems.at[5],
        (after, ch),
    )
    halo.start()
    each(0, GROUPS - 1, lambda i: scale_rows(pl.multiple_of(i * run, run), run))

    cut_one = lengths_ref[0]
    cut_two = cut_one + lengths_ref[1]
    base = ctx * tokens
    group_start = base + run * lax.broadcasted_iota(jnp.int32, (GROUPS, LANES), 0)

    def keep_at(t):
        token = group_start + t
        begins = (token == 0) | (token == cut_one) | (token == cut_two)
        return jnp.where(begins, 0.0, 1.0).astype(jnp.float32)

    def unbroken(begin, count):
        cut = (begin == 0) | ((cut_one >= begin) & (cut_one < begin + count)) | ((cut_two >= begin) & (cut_two < begin + count))
        return jnp.where(cut, 0.0, 1.0).astype(jnp.float32)

    def spread_row(values):
        return jnp.broadcast_to(values, (GROUPS, LANES))

    run_decay = [jnp.exp(-run * rates_ref[:, pl.ds(tile * LANES, LANES)]) for tile in range(tiles)]
    all_decay = [jnp.exp(-tokens * rates_ref[:, pl.ds(tile * LANES, LANES)]) for tile in range(tiles)]
    unbroken_run = [unbroken(base + run * i, run) for i in range(GROUPS)]

    unbroken_device = [unbroken(jnp.int32(device * tokens), tokens) for device in range(ctx_count)]

    def edge_to(step, tile):
        return remote(
            edge.at[ctx, tile],
            edge.at[ctx, tile],
            edge_sems.at[0, tile, step],
            edge_sems.at[1, tile, step],
            (lax.rem(ctx + step, ctx_count), ch),
        )

    def first_pass(tile):
        lanes = pl.ds(tile * LANES, LANES)
        decays = [spread_row(jnp.exp(-rates_ref[pl.ds(m, 1), lanes])) for m in range(modes)]
        taps = [
            [spread_row(taps_ref[tap, pl.ds(branch, 1), lanes]) for branch in range(BRANCHES)]
            for tap in range(TAPS)
        ]

        def collect(t, carry, decays=decays, taps=taps):
            states, one_back, two_back, keep_before, alive = carry
            keep = keep_at(t)
            far = keep * keep_before
            now = [proj[branch, tile, pl.ds(8 + t, GROUPS, stride=run), :] for branch in range(BRANCHES)]
            parts = [
                taps[0][branch] * now[branch]
                + taps[1][branch] * (keep * one_back[branch])
                + taps[2][branch] * (far * two_back[branch])
                for branch in range(BRANCHES)
            ]
            entered = parts[1] * parts[2]
            query[tile, t] = parts[0]
            gated[tile, t] = entered
            states = [decays[m] * (states[m] * keep) + entered for m in range(modes)]
            return (states, now, one_back, keep, alive * keep)

        def rows_at(t):
            return [proj[branch, tile, pl.ds(8 + t, GROUPS, stride=run), :] for branch in range(BRANCHES)]

        zero = jnp.zeros((GROUPS, LANES), jnp.float32)
        one = jnp.ones((GROUPS, LANES), jnp.float32)
        later = lax.fori_loop(
            2, run, collect, ([zero] * modes, rows_at(1), rows_at(0), keep_at(1), one), unroll=2
        )
        if tile == 0:
            halo.wait_recv()
        begun = ([zero] * modes, rows_at(-1), rows_at(-2), keep_at(-1), one)
        for t in range(2):
            begun = collect(t, begun)
        for m in range(modes):
            fall = spread_row(jnp.exp(-(run - 2.0) * rates_ref[pl.ds(m, 1), lanes]))
            ends[tile, pl.ds(m * GROUPS, GROUPS), :] = later[0][m] + fall * (later[4] * begun[0][m])
        state = jnp.zeros((modes, LANES), jnp.float32)
        for i in range(GROUPS):
            state = ends[tile, pl.ds(i, modes, stride=GROUPS), :] + (unbroken_run[i] * run_decay[tile]) * state
        edge[ctx, tile] = state
        for step in range(1, ctx_count):
            edge_to(step, tile).start()

    def multiply_out(h, g):
        parts = LANES // part_rows
        weights = w_mine[pl.ds(h * parts, parts), g // SIDE, lax.rem(g, SIDE)].reshape(LANES, features)
        out_sum[...] = out_sum[...] + jnp.dot(g_all[g, h], weights, preferred_element_type=jnp.float32)

    open_g, rest_g = plane_gather(g_all, g_send, g_recv, ctx, row, col, multiply_out)

    def second_pass(tile):
        for step in range(1, ctx_count):
            edge_to(step, tile).wait_recv()
        state = jnp.zeros((modes, LANES), jnp.float32)
        for device in range(ctx_count):
            moved = edge[device, tile] + (unbroken_device[device] * all_decay[tile]) * state
            state = jnp.where(device < ctx, moved, state)
        for i in range(GROUPS):
            starts[tile, pl.ds(i, modes, stride=GROUPS), :] = state
            if i < GROUPS - 1:
                state = ends[tile, pl.ds(i, modes, stride=GROUPS), :] + (unbroken_run[i] * run_decay[tile]) * state
        lanes = pl.ds(tile * LANES, LANES)
        decays = [spread_row(jnp.exp(-rates_ref[pl.ds(m, 1), lanes])) for m in range(modes)]
        weights = [spread_row(weight_ref[pl.ds(m, 1), lanes]) for m in range(modes)]
        direct = spread_row(skip_ref[:, lanes])

        def filtered(t, states, decays=decays, weights=weights, direct=direct):
            keep = keep_at(t)
            entered = gated[tile, t]
            states = [decays[m] * (states[m] * keep) + entered for m in range(modes)]
            terms = [weights[m] * states[m] for m in range(modes)] + [direct * entered]
            while len(terms) > 1:
                terms = [
                    terms[k] + terms[k + 1] if k + 1 < len(terms) else terms[k]
                    for k in range(0, len(terms), 2)
                ]
            mixed[tile, pl.ds(t, GROUPS, stride=run), :] = query[tile, t] * terms[0]
            return states

        lax.fori_loop(
            0, run, filtered, [starts[tile, pl.ds(m * GROUPS, GROUPS), :] for m in range(modes)], unroll=4
        )
        g_all[ch, tile] = mixed[tile].astype(jnp.bfloat16)
        open_g(tile)

    for tile in range(tiles):
        first_pass(tile)
    for step in range(1, depth_count):
        over_depth(depth_count - step).wait_recv()
        to_partner(step).start()
    for tile in range(tiles):
        second_pass(tile)

    def last_leg():
        for step in range(1, depth_count):
            to_partner(depth_count - step).wait_recv()
        to_partner(0).wait_recv()

    rest_g(last_leg, lambda: None)
    for h in range(2):
        out_ref[:, pl.ds(h * half, half)] = jnp.transpose(out_sum[pl.ds(h * half, half), :]).astype(jnp.bfloat16)

    to_next.wait_send()
    to_previous.wait_send()
    halo.wait_send()
    for step in range(1, SIDE):
        first_x(step).wait_send()
        first_y(step).wait_send()
        then_y(step).wait_send()
        then_x(step).wait_send()
    for step in range(1, depth_count):
        over_depth(step).wait_send()
    for step in range(depth_count):
        to_partner(step).wait_send()
    for step in range(1, ctx_count):
        for tile in range(tiles):
            edge_to(step, tile).wait_send()


def body(
    x_owned,
    live_blocks,
    seq_lengths,
    norm_gain,
    w_in,
    w_short,
    decay_rates,
    residues,
    skip_gain,
    w_out,
):
    ctx_count = lax.axis_size("ctx")
    ch_count = lax.axis_size("ch")
    width = norm_gain.shape[0]
    features = x_owned.shape[1]
    tokens = x_owned.shape[0] // 2
    block = tokens // 4
    half = tokens // 2
    run = tokens // GROUPS
    modes, channels = decay_rates.shape
    tiles = channels // LANES
    part_rows = channels // ctx_count
    bf16, f32 = jnp.bfloat16, jnp.float32
    smem = pl.BlockSpec(memory_space=pltpu.SMEM)
    vmem = pl.BlockSpec(memory_space=pltpu.VMEM)
    anywhere = pl.BlockSpec(memory_space=pl.ANY)
    dma = pltpu.SemaphoreType.DMA
    flops = 2 * tokens * width * BRANCHES * channels + 2 * tokens * features * ch_count * channels
    return pl.pallas_call(
        functools.partial(kernel, (ctx_count, tokens, block, width)),
        out_shape=jax.ShapeDtypeStruct((features, tokens), bf16),
        in_specs=[smem, smem] + [anywhere] * 8,
        out_specs=vmem,
        scratch_shapes=[
            pltpu.VMEM((x_owned.shape[0] + 4 * block, features), bf16),
            pltpu.VMEM((2 * block, features), bf16),
            pltpu.VMEM((ch_count, 2, half, features), bf16),
            pltpu.VMEM((BRANCHES, width, channels), bf16),
            pltpu.VMEM((BRANCHES, tokens, channels), f32),
            pltpu.VMEM((tokens, LANES), f32),
            pltpu.VMEM((BRANCHES, tiles, tokens + 8, LANES), f32),
            pltpu.VMEM((tiles, run, GROUPS, LANES), f32),
            pltpu.VMEM((tiles, run, GROUPS, LANES), f32),
            pltpu.VMEM((tiles, modes * GROUPS, LANES), f32),
            pltpu.VMEM((tiles, modes * GROUPS, LANES), f32),
            pltpu.VMEM((ctx_count, tiles, modes, LANES), f32),
            pltpu.VMEM((tiles, tokens, LANES), f32),
            pltpu.VMEM((ch_count, tiles, tokens, LANES), bf16),
            pltpu.VMEM((tokens, features), f32),
            pltpu.VMEM((SIDE, SIDE, part_rows, features), bf16),
            pltpu.VMEM((2, SIDE, SIDE, part_rows // 2, features), bf16),
            pltpu.VMEM((ctx_count, SIDE, SIDE, part_rows, features), bf16),
            pltpu.VMEM((1, width), f32),
            pltpu.VMEM((TAPS, BRANCHES, channels), f32),
            pltpu.VMEM((modes, channels), f32),
            pltpu.VMEM((modes, channels), f32),
            pltpu.VMEM((1, channels), f32),
            dma((5,)),
            dma((2 + ch_count,)),
            dma((6,)),
            dma((4, 2, SIDE)),
            dma((2, ctx_count // 2)),
            dma((2, ctx_count // 2)),
            dma((2, tiles, ctx_count)),
            dma((SIDE + 1, 2, 4)),
            dma((SIDE + 1, 2, 4)),
            dma((SIDE + 1, 2, 4)),
            dma((SIDE + 1, 2, 4)),
        ],
        compiler_params=pltpu.CompilerParams(
            collective_id=0, has_side_effects=True, vmem_limit_bytes=56 * 1024 * 1024
        ),
        cost_estimate=pl.CostEstimate(flops=flops, bytes_accessed=18 << 20, transcendentals=0),
    )(
        live_blocks,
        seq_lengths,
        norm_gain.reshape(1, width),
        w_short,
        decay_rates,
        residues,
        skip_gain.reshape(1, channels),
        x_owned,
        w_in,
        w_out,
    )


def solution(mesh):
    return jax.shard_map(
        body,
        mesh=mesh,
        in_specs=(
            P("ctx", "ch"),
            P(),
            P(),
            P(),
            P(None, None, "ch"),
            P(None, None, "ch"),
            P(None, "ch"),
            P(None, "ch"),
            P("ch"),
            P("ch", None),
        ),
        out_specs=P("ch", "ctx"),
        check_vma=False,
    )
```

```python
import functools

import jax
import jax.numpy as jnp
from jax import lax
from jax.experimental import pallas as pl
from jax.experimental.pallas import tpu as pltpu
from jax.sharding import PartitionSpec as P

EPS = 1e-06
TAPS = 3
BRANCHES = 3
SIDE = 4
LANES = 128
GROUPS = 8
MESH = pl.DeviceIdType.MESH


def remote(src, dst, send_sem, recv_sem, device):
    return pltpu.make_async_remote_copy(
        src_ref=src,
        dst_ref=dst,
        send_sem=send_sem,
        recv_sem=recv_sem,
        device_id=device,
        device_id_type=MESH,
    )


def each(lower, upper, step):
    def run(index, carry):
        step(index)
        return carry

    lax.fori_loop(lower, upper, run, 0)


def plane_gather(buf, send_sems, recv_sems, ctx, row, col, use):
    half = buf.shape[2]
    quarter = half // 2
    rows = (pl.ds(0, half), pl.ds(0, half), pl.ds(0, quarter), pl.ds(quarter, quarter))

    def place(h, first, second):
        x = lax.rem(col + (1 - h) * first + h * second + 2 * SIDE, SIDE)
        y = lax.rem(row + (1 - h) * second + h * first + 2 * SIDE, SIDE)
        return y * SIDE + x

    def offset(ring):
        k = ring - 1
        return k + k // 2 - 2 * (k // 3)

    def piece(ring, h, along):
        if isinstance(ring, int) and ring == 0:
            return place(h, along, 0)
        return place(h, offset(ring), along)

    def neighbour(ring, h, along):
        if isinstance(ring, int) and ring == 0:
            return (ctx, place(h, along, 0))
        return (ctx, place(h, 0, along))

    def copy(ring, h, kind, along):
        part = buf.at[piece(ring, h, along), h, rows[kind]]
        return remote(
            part,
            part,
            send_sems.at[ring, h, kind],
            recv_sems.at[ring, h, kind],
            neighbour(ring, h, 1 - 2 * (kind % 2)),
        )

    def send(ring, h):
        copy(ring, h, 0, 0).start()
        copy(ring, h, 1, 0).start()

    def forward(ring, h):
        copy(ring, h, 0, -1).wait_recv()
        copy(ring, h, 2, -1).start()
        copy(ring, h, 1, 1).wait_recv()
        copy(ring, h, 3, 1).start()

    def finish(ring, h):
        copy(ring, h, 2, 2).wait_recv()
        copy(ring, h, 3, 2).wait_recv()

    def open_rings(h):
        send(0, h)
        send(1, h)

    def grow(h):
        forward(0, h)
        send(2, h)
        send(3, h)

    def close_first(h):
        finish(0, h)
        send(4, h)

    def rest(opened, begun, passed):
        opened()
        each(0, 2, lambda h: use(h, place(h, 0, 0)))
        each(0, 2, grow)
        each(0, 4, lambda i: use(i // 2, piece(0, i // 2, 2 * (i % 2) - 1)))
        each(0, 2, close_first)
        each(0, 2, lambda h: use(h, piece(0, h, 2)))
        each(1, 2, pass_on)
        begun()
        each(2, SIDE + 1, pass_on)
        passed()
        each(1, SIDE + 1, take_last)
        each(0, 2, drain)

    def pass_on(ring):
        each(0, 2, lambda h: forward(ring, h))
        each(0, 4, lambda i: use(i // 2, piece(ring, i // 2, 2 * (i % 2) - 1)))

    def take_last(ring):
        each(0, 2, lambda h: finish(ring, h))
        each(0, 2, lambda h: use(h, piece(ring, h, 2)))

    def drain(index):
        h = index % 2
        for kind in range(4):
            copy(0, h, kind, 0).wait_send()
        each(1, SIDE + 1, lambda ring: drain_ring(ring, h))

    def drain_ring(ring, h):
        for kind in range(4):
            copy(ring, h, kind, 0).wait_send()

    return open_rings, rest


def kernel(
    dims,
    live_ref,
    lengths_ref,
    gain_hbm,
    taps_hbm,
    rates_hbm,
    residues_hbm,
    skip_hbm,
    x_hbm,
    w_in_hbm,
    w_out_hbm,
    out_ref,
    comb,
    last_blocks,
    x_all,
    w_in,
    sums,
    squares,
    proj,
    query,
    gated,
    ends,
    starts,
    edge,
    mixed,
    g_all,
    out_sum,
    w_stage,
    w_half,
    w_mine,
    gain_ref,
    taps_ref,
    rates_ref,
    weight_ref,
    skip_ref,
    small_sems,
    local_sems,
    shift_sems,
    split_sems,
    deep_sems,
    relay_sems,
    edge_sems,
    x_send,
    x_recv,
    g_send,
    g_recv,
):
    ctx_count, tokens, block, width = dims
    ctx = lax.axis_index("ctx")
    ch = lax.axis_index("ch")
    row = ch // SIDE
    col = lax.rem(ch, SIDE)
    partner = ctx + 1 - 2 * lax.rem(ctx, 2)
    depth_count = ctx_count // 2
    capacity = x_hbm.shape[0] // block
    own_blocks = tokens // block
    features = x_hbm.shape[1]
    part_rows = w_out_hbm.shape[0] // ctx_count
    half = tokens // 2
    modes = rates_ref.shape[0]
    small = [
        pltpu.make_async_copy(source, target, small_sems.at[i])
        for i, (source, target) in enumerate(
            (
                (gain_hbm, gain_ref),
                (taps_hbm, taps_ref),
                (rates_hbm, rates_ref),
                (residues_hbm, weight_ref),
                (skip_hbm, skip_ref),
            )
        )
    ]
    tiles = rates_ref.shape[1] // LANES
    run = tokens // GROUPS

    x_in = pltpu.make_async_copy(x_hbm, comb.at[pl.ds(0, capacity * block)], local_sems.at[0])
    x_in.start()

    def w_part(other, target, sem):
        return pltpu.make_async_copy(
            w_out_hbm.at[
                pl.ds(pl.multiple_of(ctx * part_rows, part_rows), part_rows),
                pl.ds(pl.multiple_of(other * features, features), features),
            ],
            target,
            sem,
        )

    for x in range(SIDE):
        for y in range(SIDE):
            w_part(y * SIDE + x, w_stage.at[x, y], local_sems.at[2 + x * SIDE + y]).start()
    w_load = pltpu.make_async_copy(w_in_hbm, w_in, local_sems.at[1])
    w_load.start()
    for copy in small:
        copy.start()

    barrier = pltpu.get_barrier_semaphore()
    for step in range(1, SIDE):
        pl.semaphore_signal(
            barrier, inc=1, device_id=(ctx, row * SIDE + lax.rem(col + step, SIDE)), device_id_type=MESH
        )
        pl.semaphore_signal(
            barrier, inc=1, device_id=(ctx, lax.rem(row + step, SIDE) * SIDE + col), device_id_type=MESH
        )
    for step in range(1, ctx_count):
        pl.semaphore_signal(
            barrier, inc=1, device_id=(lax.rem(ctx + step, ctx_count), ch), device_id_type=MESH
        )
    sums[...] = jnp.zeros_like(sums)
    squares[...] = jnp.zeros_like(squares)
    out_sum[...] = jnp.zeros_like(out_sum)
    x_in.wait()

    before = jnp.int32(0)
    for owner in range(ctx_count):
        before = before + jnp.where(owner < ctx, live_ref[owner], 0)
    here = live_ref[ctx]
    left_live = live_ref[lax.rem(ctx + ctx_count - 1, ctx_count)]
    first_sent = jnp.maximum(here - 2, 0)
    def pick(which, options):
        value = comb[pl.ds(options[0] * block, block), :]
        for option in options[1:]:
            value = jnp.where(which == option, comb[pl.ds(option * block, block), :], value)
        return value

    for i in range(2):
        last_blocks[pl.ds(i * block, block), :] = pick(first_sent + i, list(range(i, capacity - 1 + i)))
    pl.semaphore_wait(barrier, 2 * (SIDE - 1) + ctx_count - 1)

    after = lax.rem(ctx + 1, ctx_count)
    ahead = lax.rem(ctx + ctx_count - 1, ctx_count)
    to_next = remote(
        last_blocks,
        comb.at[pl.ds(capacity * block, 2 * block)],
        shift_sems.at[0],
        shift_sems.at[1],
        (after, ch),
    )
    to_previous = remote(
        comb.at[pl.ds(0, 2 * block)],
        comb.at[pl.ds((capacity + 2) * block, 2 * block)],
        shift_sems.at[2],
        shift_sems.at[3],
        (ahead, ch),
    )
    to_next.start()
    to_previous.start()

    upper, lower = pl.ds(0, part_rows // 2), pl.ds(part_rows // 2, part_rows // 2)
    for x in range(SIDE):
        for y in range(SIDE):
            w_part(y * SIDE + x, w_stage.at[x, y], local_sems.at[2 + x * SIDE + y]).wait()

    def first_x(step):
        x = lax.rem(col + step, SIDE)
        return remote(
            w_stage.at[x, :, upper],
            w_half.at[0, col],
            split_sems.at[0, 0, step],
            split_sems.at[0, 1, step],
            (ctx, row * SIDE + x),
        )

    def first_y(step):
        y = lax.rem(row + step, SIDE)
        return remote(
            w_stage.at[:, y, lower],
            w_half.at[1, row],
            split_sems.at[1, 0, step],
            split_sems.at[1, 1, step],
            (ctx, y * SIDE + col),
        )

    def then_y(step):
        y = lax.rem(row + step, SIDE)
        return remote(
            w_half.at[0, :, y],
            w_mine.at[ctx, row, :, upper],
            split_sems.at[2, 0, step],
            split_sems.at[2, 1, step],
            (ctx, y * SIDE + col),
        )

    def then_x(step):
        x = lax.rem(col + step, SIDE)
        return remote(
            w_half.at[1, :, x],
            w_mine.at[ctx, :, col, lower],
            split_sems.at[3, 0, step],
            split_sems.at[3, 1, step],
            (ctx, row * SIDE + x),
        )

    def over_depth(kind):
        shift = 2 * (1 - 2 * (kind % 2))
        target = lax.rem(ctx + ctx_count + shift, ctx_count)
        held = ctx if kind < 2 else lax.rem(ctx + ctx_count - shift, ctx_count)
        part = w_mine.at[held, pl.ds((0, 0, 0, SIDE // 2)[kind], (SIDE, SIDE, SIDE // 2, SIDE // 2)[kind])]
        return remote(part, part, deep_sems.at[0, kind], deep_sems.at[1, kind], (target, ch))

    def to_partner(step):
        held = lax.rem(ctx + 2 * step, ctx_count)
        return remote(
            w_mine.at[held],
            w_mine.at[held],
            relay_sems.at[0, step],
            relay_sems.at[1, step],
            (partner, ch),
        )

    for step in (1, 3, 2):
        first_x(step).start()
        first_y(step).start()
    kept = (
        pltpu.make_async_copy(w_stage.at[col, :, upper], w_half.at[0, col], local_sems.at[0]),
        pltpu.make_async_copy(w_stage.at[:, row, lower], w_half.at[1, row], local_sems.at[2]),
        pltpu.make_async_copy(w_half.at[0, :, row], w_mine.at[ctx, row, :, upper], local_sems.at[3]),
        pltpu.make_async_copy(w_half.at[1, :, col], w_mine.at[ctx, :, col, lower], local_sems.at[4]),
    )
    kept[0].start()
    kept[1].start()

    def fill(h):
        for i in range(h * own_blocks // 2, (h + 1) * own_blocks // 2):
            wanted = ctx * own_blocks + i
            local = list(range(max(i - 2, 0), min(i + 3, capacity)))
            if h == 0:
                other = capacity + left_live - (before - wanted) - jnp.maximum(left_live - 2, 0)
                source = jnp.where(wanted < before, other, wanted - before)
                options = local + [capacity, capacity + 1]
            else:
                other = capacity + 2 + wanted - before - here
                source = jnp.where(wanted >= before + here, other, wanted - before)
                options = local + [capacity + 2, capacity + 3]
            x_all[ch, h, pl.ds((i * block) % half, block), :] = pick(source, options)

    def project(h, g):
        wide = x_all[g, h].astype(jnp.float32)
        squared = wide * wide
        folded = squared[:, :LANES]
        for lane in range(1, features // LANES):
            folded = folded + squared[:, lane * LANES : (lane + 1) * LANES]
        at = pl.ds(pl.multiple_of(h * half, half), half)
        squares[at, :] = squares[at, :] + folded
        deep = pl.ds(pl.multiple_of(g * features, features), features)
        scaled = (wide * gain_ref[:, deep]).astype(jnp.bfloat16)
        for branch in range(BRANCHES):
            sums[branch, at, :] = sums[branch, at, :] + jnp.dot(
                scaled, w_in[branch, deep, :], preferred_element_type=jnp.float32
            )

    def second_leg():
        kept[0].wait()
        kept[1].wait()
        for step in range(1, SIDE):
            first_x(step).wait_recv()
            first_y(step).wait_recv()
        for step in (1, 3, 2):
            then_y(step).start()
            then_x(step).start()
        kept[2].start()
        kept[3].start()
        w_load.wait()
        for copy in small:
            copy.wait()
        doubled = 2.0 * rates_ref[...]
        series = jnp.ones_like(doubled)
        for order in range(8, 1, -1):
            series = 1.0 - doubled * (1.0 / order) * series
        risen = jnp.where(doubled < 0.1, doubled * series, 1.0 - jnp.exp(-doubled))
        weight_ref[...] = weight_ref[...] * jnp.sqrt(risen)

    def third_leg():
        for step in range(1, SIDE):
            then_y(step).wait_recv()
            then_x(step).wait_recv()
        kept[2].wait()
        kept[3].wait()
        over_depth(0).start()
        over_depth(1).start()
        to_partner(0).start()

    def fourth_leg():
        over_depth(0).wait_recv()
        over_depth(2).start()
        over_depth(1).wait_recv()
        over_depth(3).start()
        to_partner(1).start()
        to_partner(depth_count - 1).start()

    open_x, rest_x = plane_gather(x_all, x_send, x_recv, ctx, row, col, project)
    parity = lax.rem(ctx, 2)

    def take(h):
        @pl.when(h == 0)
        def _():
            to_next.wait_recv()
            fill(0)

        @pl.when(h == 1)
        def _():
            to_previous.wait_recv()
            fill(1)

        open_x(h)

    take(1 - parity)
    take(parity)
    rest_x(second_leg, third_leg, fourth_leg)
    def scale_rows(begin, count):
        total = jnp.sum(squares[pl.ds(begin, count), :], axis=1, keepdims=True)
        scale = lax.rsqrt(total / width + EPS)
        for branch in range(BRANCHES):
            for tile in range(tiles):
                proj[branch, tile, pl.ds(begin + 8, count), :] = (
                    sums[branch, pl.ds(begin, count), tile * LANES : (tile + 1) * LANES] * scale
                )

    scale_rows(tokens - run, run)
    halo = remote(
        proj.at[:, :, pl.ds(tokens, 8)],
        proj.at[:, :, pl.ds(0, 8)],
        shift_sems.at[4],
        shift_sems.at[5],
        (after, ch),
    )
    halo.start()
    each(0, GROUPS - 1, lambda i: scale_rows(pl.multiple_of(i * run, run), run))

    cut_one = lengths_ref[0]
    cut_two = cut_one + lengths_ref[1]
    base = ctx * tokens
    group_start = base + run * lax.broadcasted_iota(jnp.int32, (GROUPS, LANES), 0)

    def keep_at(t):
        token = group_start + t
        begins = (token == 0) | (token == cut_one) | (token == cut_two)
        return jnp.where(begins, 0.0, 1.0).astype(jnp.float32)

    def unbroken(begin, count):
        cut = (begin == 0) | ((cut_one >= begin) & (cut_one < begin + count)) | ((cut_two >= begin) & (cut_two < begin + count))
        return jnp.where(cut, 0.0, 1.0).astype(jnp.float32)

    def spread_row(values):
        return jnp.broadcast_to(values, (GROUPS, LANES))

    run_decay = [jnp.exp(-run * rates_ref[:, pl.ds(tile * LANES, LANES)]) for tile in range(tiles)]
    all_decay = [jnp.exp(-tokens * rates_ref[:, pl.ds(tile * LANES, LANES)]) for tile in range(tiles)]
    unbroken_run = [unbroken(base + run * i, run) for i in range(GROUPS)]

    unbroken_device = [unbroken(jnp.int32(device * tokens), tokens) for device in range(ctx_count)]

    def edge_to(step, tile):
        return remote(
            edge.at[ctx, tile],
            edge.at[ctx, tile],
            edge_sems.at[0, tile, step],
            edge_sems.at[1, tile, step],
            (lax.rem(ctx + step, ctx_count), ch),
        )

    def first_pass(tile):
        lanes = pl.ds(tile * LANES, LANES)
        decays = [spread_row(jnp.exp(-rates_ref[pl.ds(m, 1), lanes])) for m in range(modes)]
        taps = [
            [spread_row(taps_ref[tap, pl.ds(branch, 1), lanes]) for branch in range(BRANCHES)]
            for tap in range(TAPS)
        ]

        def collect(t, carry, decays=decays, taps=taps):
            states, one_back, two_back, keep_before, alive = carry
            keep = keep_at(t)
            far = keep * keep_before
            now = [proj[branch, tile, pl.ds(8 + t, GROUPS, stride=run), :] for branch in range(BRANCHES)]
            parts = [
                taps[0][branch] * now[branch]
                + taps[1][branch] * (keep * one_back[branch])
                + taps[2][branch] * (far * two_back[branch])
                for branch in range(BRANCHES)
            ]
            entered = parts[1] * parts[2]
            query[tile, t] = parts[0]
            gated[tile, t] = entered
            states = [decays[m] * (states[m] * keep) + entered for m in range(modes)]
            return (states, now, one_back, keep, alive * keep)

        def rows_at(t):
            return [proj[branch, tile, pl.ds(8 + t, GROUPS, stride=run), :] for branch in range(BRANCHES)]

        zero = jnp.zeros((GROUPS, LANES), jnp.float32)
        one = jnp.ones((GROUPS, LANES), jnp.float32)
        later = lax.fori_loop(
            2, run, collect, ([zero] * modes, rows_at(1), rows_at(0), keep_at(1), one), unroll=2
        )
        if tile == 0:
            halo.wait_recv()
        begun = ([zero] * modes, rows_at(-1), rows_at(-2), keep_at(-1), one)
        for t in range(2):
            begun = collect(t, begun)
        for m in range(modes):
            fall = spread_row(jnp.exp(-(run - 2.0) * rates_ref[pl.ds(m, 1), lanes]))
            ends[tile, pl.ds(m * GROUPS, GROUPS), :] = later[0][m] + fall * (later[4] * begun[0][m])
        state = jnp.zeros((modes, LANES), jnp.float32)
        for i in range(GROUPS):
            state = ends[tile, pl.ds(i, modes, stride=GROUPS), :] + (unbroken_run[i] * run_decay[tile]) * state
        edge[ctx, tile] = state
        for step in range(1, ctx_count):
            edge_to(step, tile).start()

    def multiply_out(h, g):
        parts = LANES // part_rows
        weights = w_mine[pl.ds(h * parts, parts), g // SIDE, lax.rem(g, SIDE)].reshape(LANES, features)
        out_sum[...] = out_sum[...] + jnp.dot(g_all[g, h], weights, preferred_element_type=jnp.float32)

    open_g, rest_g = plane_gather(g_all, g_send, g_recv, ctx, row, col, multiply_out)

    def second_pass(tile):
        for step in range(1, ctx_count):
            edge_to(step, tile).wait_recv()
        state = jnp.zeros((modes, LANES), jnp.float32)
        for device in range(ctx_count):
            moved = edge[device, tile] + (unbroken_device[device] * all_decay[tile]) * state
            state = jnp.where(device < ctx, moved, state)
        for i in range(GROUPS):
            starts[tile, pl.ds(i, modes, stride=GROUPS), :] = state
            if i < GROUPS - 1:
                state = ends[tile, pl.ds(i, modes, stride=GROUPS), :] + (unbroken_run[i] * run_decay[tile]) * state
        lanes = pl.ds(tile * LANES, LANES)
        decays = [spread_row(jnp.exp(-rates_ref[pl.ds(m, 1), lanes])) for m in range(modes)]
        weights = [spread_row(weight_ref[pl.ds(m, 1), lanes]) for m in range(modes)]
        direct = spread_row(skip_ref[:, lanes])

        def filtered(t, states, decays=decays, weights=weights, direct=direct):
            keep = keep_at(t)
            entered = gated[tile, t]
            states = [decays[m] * (states[m] * keep) + entered for m in range(modes)]
            terms = [weights[m] * states[m] for m in range(modes)] + [direct * entered]
            while len(terms) > 1:
                terms = [
                    terms[k] + terms[k + 1] if k + 1 < len(terms) else terms[k]
                    for k in range(0, len(terms), 2)
                ]
            mixed[tile, pl.ds(t, GROUPS, stride=run), :] = query[tile, t] * terms[0]
            return states

        lax.fori_loop(
            0, run, filtered, [starts[tile, pl.ds(m * GROUPS, GROUPS), :] for m in range(modes)], unroll=4
        )
        g_all[ch, tile] = mixed[tile].astype(jnp.bfloat16)
        open_g(tile)

    for tile in range(tiles):
        first_pass(tile)
    over_depth(2).wait_recv()
    over_depth(3).wait_recv()
    to_partner(2).start()
    for tile in range(tiles):
        second_pass(tile)

    def last_leg():
        for step in range(1, depth_count):
            to_partner(depth_count - step).wait_recv()
        to_partner(0).wait_recv()

    rest_g(last_leg, lambda: None, lambda: None)
    for h in range(2):
        out_ref[:, pl.ds(h * half, half)] = jnp.transpose(out_sum[pl.ds(h * half, half), :]).astype(jnp.bfloat16)

    to_next.wait_send()
    to_previous.wait_send()
    halo.wait_send()
    for step in range(1, SIDE):
        first_x(step).wait_send()
        first_y(step).wait_send()
        then_y(step).wait_send()
        then_x(step).wait_send()
    for kind in range(4):
        over_depth(kind).wait_send()
    for step in range(depth_count):
        to_partner(step).wait_send()
    for step in range(1, ctx_count):
        for tile in range(tiles):
            edge_to(step, tile).wait_send()


def body(
    x_owned,
    live_blocks,
    seq_lengths,
    norm_gain,
    w_in,
    w_short,
    decay_rates,
    residues,
    skip_gain,
    w_out,
):
    ctx_count = lax.axis_size("ctx")
    ch_count = lax.axis_size("ch")
    width = norm_gain.shape[0]
    features = x_owned.shape[1]
    tokens = x_owned.shape[0] // 2
    block = tokens // 4
    half = tokens // 2
    run = tokens // GROUPS
    modes, channels = decay_rates.shape
    tiles = channels // LANES
    part_rows = channels // ctx_count
    bf16, f32 = jnp.bfloat16, jnp.float32
    smem = pl.BlockSpec(memory_space=pltpu.SMEM)
    vmem = pl.BlockSpec(memory_space=pltpu.VMEM)
    anywhere = pl.BlockSpec(memory_space=pl.ANY)
    dma = pltpu.SemaphoreType.DMA
    flops = 2 * tokens * width * BRANCHES * channels + 2 * tokens * features * ch_count * channels
    return pl.pallas_call(
        functools.partial(kernel, (ctx_count, tokens, block, width)),
        out_shape=jax.ShapeDtypeStruct((features, tokens), bf16),
        in_specs=[smem, smem] + [anywhere] * 8,
        out_specs=vmem,
        scratch_shapes=[
            pltpu.VMEM((x_owned.shape[0] + 4 * block, features), bf16),
            pltpu.VMEM((2 * block, features), bf16),
            pltpu.VMEM((ch_count, 2, half, features), bf16),
            pltpu.VMEM((BRANCHES, width, channels), bf16),
            pltpu.VMEM((BRANCHES, tokens, channels), f32),
            pltpu.VMEM((tokens, LANES), f32),
            pltpu.VMEM((BRANCHES, tiles, tokens + 8, LANES), f32),
            pltpu.VMEM((tiles, run, GROUPS, LANES), f32),
            pltpu.VMEM((tiles, run, GROUPS, LANES), f32),
            pltpu.VMEM((tiles, modes * GROUPS, LANES), f32),
            pltpu.VMEM((tiles, modes * GROUPS, LANES), f32),
            pltpu.VMEM((ctx_count, tiles, modes, LANES), f32),
            pltpu.VMEM((tiles, tokens, LANES), f32),
            pltpu.VMEM((ch_count, tiles, tokens, LANES), bf16),
            pltpu.VMEM((tokens, features), f32),
            pltpu.VMEM((SIDE, SIDE, part_rows, features), bf16),
            pltpu.VMEM((2, SIDE, SIDE, part_rows // 2, features), bf16),
            pltpu.VMEM((ctx_count, SIDE, SIDE, part_rows, features), bf16),
            pltpu.VMEM((1, width), f32),
            pltpu.VMEM((TAPS, BRANCHES, channels), f32),
            pltpu.VMEM((modes, channels), f32),
            pltpu.VMEM((modes, channels), f32),
            pltpu.VMEM((1, channels), f32),
            dma((5,)),
            dma((2 + ch_count,)),
            dma((6,)),
            dma((4, 2, SIDE)),
            dma((2, 4)),
            dma((2, ctx_count // 2)),
            dma((2, tiles, ctx_count)),
            dma((SIDE + 1, 2, 4)),
            dma((SIDE + 1, 2, 4)),
            dma((SIDE + 1, 2, 4)),
            dma((SIDE + 1, 2, 4)),
        ],
        compiler_params=pltpu.CompilerParams(
            collective_id=0, has_side_effects=True, vmem_limit_bytes=56 * 1024 * 1024
        ),
        cost_estimate=pl.CostEstimate(flops=flops, bytes_accessed=18 << 20, transcendentals=0),
    )(
        live_blocks,
        seq_lengths,
        norm_gain.reshape(1, width),
        w_short,
        decay_rates,
        residues,
        skip_gain.reshape(1, channels),
        x_owned,
        w_in,
        w_out,
    )


def solution(mesh):
    return jax.shard_map(
        body,
        mesh=mesh,
        in_specs=(
            P("ctx", "ch"),
            P(),
            P(),
            P(),
            P(None, None, "ch"),
            P(None, None, "ch"),
            P(None, "ch"),
            P(None, "ch"),
            P("ch"),
            P("ch", None),
        ),
        out_specs=P("ch", "ctx"),
        check_vma=False,
    )
```

```python
import functools

import jax
import jax.numpy as jnp
from jax import lax
from jax.experimental import pallas as pl
from jax.experimental.pallas import tpu as pltpu
from jax.sharding import PartitionSpec as P

EPS = 1e-06
TAPS = 3
BRANCHES = 3
SIDE = 4
LANES = 128
GROUPS = 8
MESH = pl.DeviceIdType.MESH


def remote(src, dst, send_sem, recv_sem, device):
    return pltpu.make_async_remote_copy(
        src_ref=src,
        dst_ref=dst,
        send_sem=send_sem,
        recv_sem=recv_sem,
        device_id=device,
        device_id_type=MESH,
    )


def each(lower, upper, step):
    def run(index, carry):
        step(index)
        return carry

    lax.fori_loop(lower, upper, run, 0)


def plane_gather(buf, send_sems, recv_sems, ctx, row, col, use):
    half = buf.shape[2]
    quarter = half // 2
    rows = (pl.ds(0, half), pl.ds(0, half), pl.ds(0, quarter), pl.ds(quarter, quarter))

    def place(h, first, second):
        x = lax.rem(col + (1 - h) * first + h * second + 2 * SIDE, SIDE)
        y = lax.rem(row + (1 - h) * second + h * first + 2 * SIDE, SIDE)
        return y * SIDE + x

    def offset(ring):
        k = ring - 1
        return k + k // 2 - 2 * (k // 3)

    def piece(ring, h, along):
        if isinstance(ring, int) and ring == 0:
            return place(h, along, 0)
        return place(h, offset(ring), along)

    def neighbour(ring, h, along):
        if isinstance(ring, int) and ring == 0:
            return (ctx, place(h, along, 0))
        return (ctx, place(h, 0, along))

    def copy(ring, h, kind, along):
        part = buf.at[piece(ring, h, along), h, rows[kind]]
        return remote(
            part,
            part,
            send_sems.at[ring, h, kind],
            recv_sems.at[ring, h, kind],
            neighbour(ring, h, 1 - 2 * (kind % 2)),
        )

    def send(ring, h):
        copy(ring, h, 0, 0).start()
        copy(ring, h, 1, 0).start()

    def forward(ring, h):
        copy(ring, h, 0, -1).wait_recv()
        copy(ring, h, 2, -1).start()
        copy(ring, h, 1, 1).wait_recv()
        copy(ring, h, 3, 1).start()

    def finish(ring, h):
        copy(ring, h, 2, 2).wait_recv()
        copy(ring, h, 3, 2).wait_recv()

    def open_rings(h):
        send(0, h)
        send(1, h)

    def grow(h):
        forward(0, h)
        send(2, h)
        send(3, h)

    def close_first(h):
        finish(0, h)
        send(4, h)

    def rest(opened, grown):
        opened()
        each(0, 2, lambda h: use(h, place(h, 0, 0)))
        each(0, 2, grow)
        grown()
        each(0, 4, lambda i: use(i // 2, piece(0, i // 2, 2 * (i % 2) - 1)))
        each(0, 2, close_first)
        each(0, 2, lambda h: use(h, piece(0, h, 2)))
        each(1, SIDE + 1, pass_on)
        each(1, SIDE + 1, take_last)
        each(0, 2, drain)

    def pass_on(ring):
        each(0, 2, lambda h: forward(ring, h))
        each(0, 4, lambda i: use(i // 2, piece(ring, i // 2, 2 * (i % 2) - 1)))

    def take_last(ring):
        each(0, 2, lambda h: finish(ring, h))
        each(0, 2, lambda h: use(h, piece(ring, h, 2)))

    def drain(index):
        h = index % 2
        for kind in range(4):
            copy(0, h, kind, 0).wait_send()
        each(1, SIDE + 1, lambda ring: drain_ring(ring, h))

    def drain_ring(ring, h):
        for kind in range(4):
            copy(ring, h, kind, 0).wait_send()

    return open_rings, rest


def kernel(
    dims,
    live_ref,
    lengths_ref,
    gain_hbm,
    taps_hbm,
    rates_hbm,
    residues_hbm,
    skip_hbm,
    x_hbm,
    w_in_hbm,
    w_out_hbm,
    out_ref,
    comb,
    last_blocks,
    x_all,
    w_in,
    sums,
    squares,
    proj,
    query,
    gated,
    ends,
    starts,
    edge,
    mixed,
    g_all,
    out_sum,
    w_stage,
    w_half,
    w_mine,
    gain_ref,
    taps_ref,
    rates_ref,
    weight_ref,
    skip_ref,
    small_sems,
    local_sems,
    shift_sems,
    split_sems,
    deep_sems,
    relay_sems,
    edge_sems,
    x_send,
    x_recv,
    g_send,
    g_recv,
):
    ctx_count, tokens, block, width = dims
    ctx = lax.axis_index("ctx")
    ch = lax.axis_index("ch")
    row = ch // SIDE
    col = lax.rem(ch, SIDE)
    partner = ctx + 1 - 2 * lax.rem(ctx, 2)
    depth_count = ctx_count // 2
    capacity = x_hbm.shape[0] // block
    own_blocks = tokens // block
    features = x_hbm.shape[1]
    part_rows = w_out_hbm.shape[0] // ctx_count
    half = tokens // 2
    modes = rates_ref.shape[0]
    small = [
        pltpu.make_async_copy(source, target, small_sems.at[i])
        for i, (source, target) in enumerate(
            (
                (gain_hbm, gain_ref),
                (taps_hbm, taps_ref),
                (rates_hbm, rates_ref),
                (residues_hbm, weight_ref),
                (skip_hbm, skip_ref),
            )
        )
    ]
    tiles = rates_ref.shape[1] // LANES
    run = tokens // GROUPS

    x_in = pltpu.make_async_copy(x_hbm, comb.at[pl.ds(0, capacity * block)], local_sems.at[0])
    x_in.start()

    def w_part(other, target, sem):
        return pltpu.make_async_copy(
            w_out_hbm.at[
                pl.ds(pl.multiple_of(ctx * part_rows, part_rows), part_rows),
                pl.ds(pl.multiple_of(other * features, features), features),
            ],
            target,
            sem,
        )

    for x in range(SIDE):
        for y in range(SIDE):
            w_part(y * SIDE + x, w_stage.at[x, y], local_sems.at[2 + x * SIDE + y]).start()
    w_load = pltpu.make_async_copy(w_in_hbm, w_in, local_sems.at[1])
    w_load.start()
    for copy in small:
        copy.start()

    barrier = pltpu.get_barrier_semaphore()
    for step in range(1, SIDE):
        pl.semaphore_signal(
            barrier, inc=1, device_id=(ctx, row * SIDE + lax.rem(col + step, SIDE)), device_id_type=MESH
        )
        pl.semaphore_signal(
            barrier, inc=1, device_id=(ctx, lax.rem(row + step, SIDE) * SIDE + col), device_id_type=MESH
        )
    for step in range(1, ctx_count):
        pl.semaphore_signal(
            barrier, inc=1, device_id=(lax.rem(ctx + step, ctx_count), ch), device_id_type=MESH
        )
    sums[...] = jnp.zeros_like(sums)
    squares[...] = jnp.zeros_like(squares)
    out_sum[...] = jnp.zeros_like(out_sum)
    x_in.wait()

    before = jnp.int32(0)
    for owner in range(ctx_count):
        before = before + jnp.where(owner < ctx, live_ref[owner], 0)
    here = live_ref[ctx]
    left_live = live_ref[lax.rem(ctx + ctx_count - 1, ctx_count)]
    first_sent = jnp.maximum(here - 2, 0)
    def pick(which, options):
        value = comb[pl.ds(options[0] * block, block), :]
        for option in options[1:]:
            value = jnp.where(which == option, comb[pl.ds(option * block, block), :], value)
        return value

    for i in range(2):
        last_blocks[pl.ds(i * block, block), :] = pick(first_sent + i, list(range(i, capacity - 1 + i)))
    pl.semaphore_wait(barrier, 2 * (SIDE - 1) + ctx_count - 1)

    after = lax.rem(ctx + 1, ctx_count)
    ahead = lax.rem(ctx + ctx_count - 1, ctx_count)
    to_next = remote(
        last_blocks,
        comb.at[pl.ds(capacity * block, 2 * block)],
        shift_sems.at[0],
        shift_sems.at[1],
        (after, ch),
    )
    to_previous = remote(
        comb.at[pl.ds(0, 2 * block)],
        comb.at[pl.ds((capacity + 2) * block, 2 * block)],
        shift_sems.at[2],
        shift_sems.at[3],
        (ahead, ch),
    )
    to_next.start()
    to_previous.start()

    upper, lower = pl.ds(0, part_rows // 2), pl.ds(part_rows // 2, part_rows // 2)
    for x in range(SIDE):
        for y in range(SIDE):
            w_part(y * SIDE + x, w_stage.at[x, y], local_sems.at[2 + x * SIDE + y]).wait()

    def first_x(step):
        x = lax.rem(col + step, SIDE)
        return remote(
            w_stage.at[x, :, upper],
            w_half.at[0, col],
            split_sems.at[0, 0, step],
            split_sems.at[0, 1, step],
            (ctx, row * SIDE + x),
        )

    def first_y(step):
        y = lax.rem(row + step, SIDE)
        return remote(
            w_stage.at[:, y, lower],
            w_half.at[1, row],
            split_sems.at[1, 0, step],
            split_sems.at[1, 1, step],
            (ctx, y * SIDE + col),
        )

    def then_y(step):
        y = lax.rem(row + step, SIDE)
        return remote(
            w_half.at[0, :, y],
            w_mine.at[ctx, row, :, upper],
            split_sems.at[2, 0, step],
            split_sems.at[2, 1, step],
            (ctx, y * SIDE + col),
        )

    def then_x(step):
        x = lax.rem(col + step, SIDE)
        return remote(
            w_half.at[1, :, x],
            w_mine.at[ctx, :, col, lower],
            split_sems.at[3, 0, step],
            split_sems.at[3, 1, step],
            (ctx, row * SIDE + x),
        )

    def over_depth(step):
        return remote(
            w_mine.at[ctx],
            w_mine.at[ctx],
            deep_sems.at[0, step],
            deep_sems.at[1, step],
            (lax.rem(ctx + 2 * step, ctx_count), ch),
        )

    def to_partner(step):
        held = lax.rem(ctx + 2 * step, ctx_count)
        return remote(
            w_mine.at[held],
            w_mine.at[held],
            relay_sems.at[0, step],
            relay_sems.at[1, step],
            (partner, ch),
        )

    for step in (1, 3, 2):
        first_x(step).start()
        first_y(step).start()
    kept = (
        pltpu.make_async_copy(w_stage.at[col, :, upper], w_half.at[0, col], local_sems.at[0]),
        pltpu.make_async_copy(w_stage.at[:, row, lower], w_half.at[1, row], local_sems.at[2]),
        pltpu.make_async_copy(w_half.at[0, :, row], w_mine.at[ctx, row, :, upper], local_sems.at[3]),
        pltpu.make_async_copy(w_half.at[1, :, col], w_mine.at[ctx, :, col, lower], local_sems.at[4]),
    )
    kept[0].start()
    kept[1].start()

    def fill(h):
        for i in range(h * own_blocks // 2, (h + 1) * own_blocks // 2):
            wanted = ctx * own_blocks + i
            local = list(range(max(i - 2, 0), min(i + 3, capacity)))
            if h == 0:
                other = capacity + left_live - (before - wanted) - jnp.maximum(left_live - 2, 0)
                source = jnp.where(wanted < before, other, wanted - before)
                options = local + [capacity, capacity + 1]
            else:
                other = capacity + 2 + wanted - before - here
                source = jnp.where(wanted >= before + here, other, wanted - before)
                options = local + [capacity + 2, capacity + 3]
            x_all[ch, h, pl.ds((i * block) % half, block), :] = pick(source, options)

    def project(h, g):
        wide = x_all[g, h].astype(jnp.float32)
        squared = wide * wide
        folded = squared[:, :LANES]
        for lane in range(1, features // LANES):
            folded = folded + squared[:, lane * LANES : (lane + 1) * LANES]
        at = pl.ds(pl.multiple_of(h * half, half), half)
        squares[at, :] = squares[at, :] + folded
        deep = pl.ds(pl.multiple_of(g * features, features), features)
        scaled = (wide * gain_ref[:, deep]).astype(jnp.bfloat16)
        for branch in range(BRANCHES):
            sums[branch, at, :] = sums[branch, at, :] + jnp.dot(
                scaled, w_in[branch, deep, :], preferred_element_type=jnp.float32
            )

    def second_leg():
        kept[0].wait()
        kept[1].wait()
        for step in range(1, SIDE):
            first_x(step).wait_recv()
            first_y(step).wait_recv()
        for step in (1, 3, 2):
            then_y(step).start()
            then_x(step).start()
        kept[2].start()
        kept[3].start()
        w_load.wait()
        for copy in small:
            copy.wait()
        doubled = 2.0 * rates_ref[...]
        series = jnp.ones_like(doubled)
        for order in range(8, 1, -1):
            series = 1.0 - doubled * (1.0 / order) * series
        risen = jnp.where(doubled < 0.1, doubled * series, 1.0 - jnp.exp(-doubled))
        weight_ref[...] = weight_ref[...] * jnp.sqrt(risen)

    def third_leg():
        for step in range(1, SIDE):
            then_y(step).wait_recv()
            then_x(step).wait_recv()
        kept[2].wait()
        kept[3].wait()
        for step in range(1, depth_count):
            over_depth(step).start()
        to_partner(0).start()

    open_x, rest_x = plane_gather(x_all, x_send, x_recv, ctx, row, col, project)
    parity = lax.rem(ctx, 2)

    def take(h):
        @pl.when(h == 0)
        def _():
            to_next.wait_recv()
            fill(0)

        @pl.when(h == 1)
        def _():
            to_previous.wait_recv()
            fill(1)

        open_x(h)

    take(1 - parity)
    take(parity)
    rest_x(second_leg, third_leg)
    def scale_rows(begin, count):
        total = jnp.sum(squares[pl.ds(begin, count), :], axis=1, keepdims=True)
        scale = lax.rsqrt(total / width + EPS)
        for branch in range(BRANCHES):
            for tile in range(tiles):
                proj[branch, tile, pl.ds(begin + 8, count), :] = (
                    sums[branch, pl.ds(begin, count), tile * LANES : (tile + 1) * LANES] * scale
                )

    scale_rows(tokens - run, run)
    halo = remote(
        proj.at[:, :, pl.ds(tokens, 8)],
        proj.at[:, :, pl.ds(0, 8)],
        shift_sems.at[4],
        shift_sems.at[5],
        (after, ch),
    )
    halo.start()
    each(0, GROUPS - 1, lambda i: scale_rows(pl.multiple_of(i * run, run), run))

    cut_one = lengths_ref[0]
    cut_two = cut_one + lengths_ref[1]
    base = ctx * tokens
    group_start = base + run * lax.broadcasted_iota(jnp.int32, (GROUPS, LANES), 0)

    def keep_at(t):
        token = group_start + t
        begins = (token == 0) | (token == cut_one) | (token == cut_two)
        return jnp.where(begins, 0.0, 1.0).astype(jnp.float32)

    def unbroken(begin, count):
        cut = (begin == 0) | ((cut_one >= begin) & (cut_one < begin + count)) | ((cut_two >= begin) & (cut_two < begin + count))
        return jnp.where(cut, 0.0, 1.0).astype(jnp.float32)

    def spread_row(values):
        return jnp.broadcast_to(values, (GROUPS, LANES))

    run_decay = [jnp.exp(-run * rates_ref[:, pl.ds(tile * LANES, LANES)]) for tile in range(tiles)]
    all_decay = [jnp.exp(-tokens * rates_ref[:, pl.ds(tile * LANES, LANES)]) for tile in range(tiles)]
    unbroken_run = [unbroken(base + run * i, run) for i in range(GROUPS)]

    unbroken_device = [unbroken(jnp.int32(device * tokens), tokens) for device in range(ctx_count)]

    def edge_to(step, tile):
        return remote(
            edge.at[ctx, tile],
            edge.at[ctx, tile],
            edge_sems.at[0, tile, step],
            edge_sems.at[1, tile, step],
            (lax.rem(ctx + step, ctx_count), ch),
        )

    def first_pass(tile):
        lanes = pl.ds(tile * LANES, LANES)
        decays = [spread_row(jnp.exp(-rates_ref[pl.ds(m, 1), lanes])) for m in range(modes)]
        taps = [
            [spread_row(taps_ref[tap, pl.ds(branch, 1), lanes]) for branch in range(BRANCHES)]
            for tap in range(TAPS)
        ]

        def collect(t, carry, decays=decays, taps=taps):
            states, one_back, two_back, keep_before, alive = carry
            keep = keep_at(t)
            far = keep * keep_before
            now = [proj[branch, tile, pl.ds(8 + t, GROUPS, stride=run), :] for branch in range(BRANCHES)]
            parts = [
                taps[0][branch] * now[branch]
                + taps[1][branch] * (keep * one_back[branch])
                + taps[2][branch] * (far * two_back[branch])
                for branch in range(BRANCHES)
            ]
            entered = parts[1] * parts[2]
            query[tile, t] = parts[0]
            gated[tile, t] = entered
            states = [decays[m] * (states[m] * keep) + entered for m in range(modes)]
            return (states, now, one_back, keep, alive * keep)

        def rows_at(t):
            return [proj[branch, tile, pl.ds(8 + t, GROUPS, stride=run), :] for branch in range(BRANCHES)]

        zero = jnp.zeros((GROUPS, LANES), jnp.float32)
        one = jnp.ones((GROUPS, LANES), jnp.float32)
        later = lax.fori_loop(
            2, run, collect, ([zero] * modes, rows_at(1), rows_at(0), keep_at(1), one), unroll=2
        )
        if tile == 0:
            halo.wait_recv()
        begun = ([zero] * modes, rows_at(-1), rows_at(-2), keep_at(-1), one)
        for t in range(2):
            begun = collect(t, begun)
        for m in range(modes):
            fall = spread_row(jnp.exp(-(run - 2.0) * rates_ref[pl.ds(m, 1), lanes]))
            ends[tile, pl.ds(m * GROUPS, GROUPS), :] = later[0][m] + fall * (later[4] * begun[0][m])
        state = jnp.zeros((modes, LANES), jnp.float32)
        for i in range(GROUPS):
            state = ends[tile, pl.ds(i, modes, stride=GROUPS), :] + (unbroken_run[i] * run_decay[tile]) * state
        edge[ctx, tile] = state
        for step in range(1, ctx_count):
            edge_to(step, tile).start()

    def multiply_out(h, g):
        parts = LANES // part_rows
        weights = w_mine[pl.ds(h * parts, parts), g // SIDE, lax.rem(g, SIDE)].reshape(LANES, features)
        out_sum[...] = out_sum[...] + jnp.dot(g_all[g, h], weights, preferred_element_type=jnp.float32)

    open_g, rest_g = plane_gather(g_all, g_send, g_recv, ctx, row, col, multiply_out)

    def second_pass(tile):
        for step in range(1, ctx_count):
            edge_to(step, tile).wait_recv()
        state = jnp.zeros((modes, LANES), jnp.float32)
        for device in range(ctx_count):
            moved = edge[device, tile] + (unbroken_device[device] * all_decay[tile]) * state
            state = jnp.where(device < ctx, moved, state)
        for i in range(GROUPS):
            starts[tile, pl.ds(i, modes, stride=GROUPS), :] = state
            if i < GROUPS - 1:
                state = ends[tile, pl.ds(i, modes, stride=GROUPS), :] + (unbroken_run[i] * run_decay[tile]) * state
        lanes = pl.ds(tile * LANES, LANES)
        decays = [spread_row(jnp.exp(-rates_ref[pl.ds(m, 1), lanes])) for m in range(modes)]
        weights = [spread_row(weight_ref[pl.ds(m, 1), lanes]) for m in range(modes)]
        direct = spread_row(skip_ref[:, lanes])

        def filtered(t, states, decays=decays, weights=weights, direct=direct):
            keep = keep_at(t)
            entered = gated[tile, t]
            states = [decays[m] * (states[m] * keep) + entered for m in range(modes)]
            terms = [weights[m] * states[m] for m in range(modes)] + [direct * entered]
            while len(terms) > 1:
                terms = [
                    terms[k] + terms[k + 1] if k + 1 < len(terms) else terms[k]
                    for k in range(0, len(terms), 2)
                ]
            mixed[tile, pl.ds(t, GROUPS, stride=run), :] = query[tile, t] * terms[0]
            return states

        lax.fori_loop(
            0, run, filtered, [starts[tile, pl.ds(m * GROUPS, GROUPS), :] for m in range(modes)], unroll=4
        )
        g_all[ch, tile] = mixed[tile].astype(jnp.bfloat16)
        open_g(tile)

    for tile in range(tiles):
        first_pass(tile)
    for step in range(1, depth_count):
        over_depth(depth_count - step).wait_recv()
        to_partner(step).start()
    for tile in range(tiles):
        second_pass(tile)

    def last_leg():
        for step in range(1, depth_count):
            to_partner(depth_count - step).wait_recv()
        to_partner(0).wait_recv()

    rest_g(last_leg, lambda: None)
    out_ref[...] = out_sum[...].astype(jnp.bfloat16)

    to_next.wait_send()
    to_previous.wait_send()
    halo.wait_send()
    for step in range(1, SIDE):
        first_x(step).wait_send()
        first_y(step).wait_send()
        then_y(step).wait_send()
        then_x(step).wait_send()
    for step in range(1, depth_count):
        over_depth(step).wait_send()
    for step in range(depth_count):
        to_partner(step).wait_send()
    for step in range(1, ctx_count):
        for tile in range(tiles):
            edge_to(step, tile).wait_send()


def body(
    x_owned,
    live_blocks,
    seq_lengths,
    norm_gain,
    w_in,
    w_short,
    decay_rates,
    residues,
    skip_gain,
    w_out,
):
    ctx_count = lax.axis_size("ctx")
    ch_count = lax.axis_size("ch")
    width = norm_gain.shape[0]
    features = x_owned.shape[1]
    tokens = x_owned.shape[0] // 2
    block = tokens // 4
    half = tokens // 2
    run = tokens // GROUPS
    modes, channels = decay_rates.shape
    tiles = channels // LANES
    part_rows = channels // ctx_count
    bf16, f32 = jnp.bfloat16, jnp.float32
    smem = pl.BlockSpec(memory_space=pltpu.SMEM)
    vmem = pl.BlockSpec(memory_space=pltpu.VMEM)
    anywhere = pl.BlockSpec(memory_space=pl.ANY)
    dma = pltpu.SemaphoreType.DMA
    flops = 2 * tokens * width * BRANCHES * channels + 2 * tokens * features * ch_count * channels
    by_token = pl.pallas_call(
        functools.partial(kernel, (ctx_count, tokens, block, width)),
        out_shape=jax.ShapeDtypeStruct((tokens, features), bf16),
        in_specs=[smem, smem] + [anywhere] * 8,
        out_specs=vmem,
        scratch_shapes=[
            pltpu.VMEM((x_owned.shape[0] + 4 * block, features), bf16),
            pltpu.VMEM((2 * block, features), bf16),
            pltpu.VMEM((ch_count, 2, half, features), bf16),
            pltpu.VMEM((BRANCHES, width, channels), bf16),
            pltpu.VMEM((BRANCHES, tokens, channels), f32),
            pltpu.VMEM((tokens, LANES), f32),
            pltpu.VMEM((BRANCHES, tiles, tokens + 8, LANES), f32),
            pltpu.VMEM((tiles, run, GROUPS, LANES), f32),
            pltpu.VMEM((tiles, run, GROUPS, LANES), f32),
            pltpu.VMEM((tiles, modes * GROUPS, LANES), f32),
            pltpu.VMEM((tiles, modes * GROUPS, LANES), f32),
            pltpu.VMEM((ctx_count, tiles, modes, LANES), f32),
            pltpu.VMEM((tiles, tokens, LANES), f32),
            pltpu.VMEM((ch_count, tiles, tokens, LANES), bf16),
            pltpu.VMEM((tokens, features), f32),
            pltpu.VMEM((SIDE, SIDE, part_rows, features), bf16),
            pltpu.VMEM((2, SIDE, SIDE, part_rows // 2, features), bf16),
            pltpu.VMEM((ctx_count, SIDE, SIDE, part_rows, features), bf16),
            pltpu.VMEM((1, width), f32),
            pltpu.VMEM((TAPS, BRANCHES, channels), f32),
            pltpu.VMEM((modes, channels), f32),
            pltpu.VMEM((modes, channels), f32),
            pltpu.VMEM((1, channels), f32),
            dma((5,)),
            dma((2 + ch_count,)),
            dma((6,)),
            dma((4, 2, SIDE)),
            dma((2, ctx_count // 2)),
            dma((2, ctx_count // 2)),
            dma((2, tiles, ctx_count)),
            dma((SIDE + 1, 2, 4)),
            dma((SIDE + 1, 2, 4)),
            dma((SIDE + 1, 2, 4)),
            dma((SIDE + 1, 2, 4)),
        ],
        compiler_params=pltpu.CompilerParams(
            collective_id=0, has_side_effects=True, vmem_limit_bytes=56 * 1024 * 1024
        ),
        cost_estimate=pl.CostEstimate(flops=flops, bytes_accessed=18 << 20, transcendentals=0),
    )(
        live_blocks,
        seq_lengths,
        norm_gain.reshape(1, width),
        w_short,
        decay_rates,
        residues,
        skip_gain.reshape(1, channels),
        x_owned,
        w_in,
        w_out,
    )
    return by_token.T


def solution(mesh):
    return jax.shard_map(
        body,
        mesh=mesh,
        in_specs=(
            P("ctx", "ch"),
            P(),
            P(),
            P(),
            P(None, None, "ch"),
            P(None, None, "ch"),
            P(None, "ch"),
            P(None, "ch"),
            P("ch"),
            P("ch", None),
        ),
        out_specs=P("ch", "ctx"),
        check_vma=False,
    )
```
